128 devices in a mesh: fsdp: 32 (over z_lo, x, y), dp: 4 (over z_hi, core).
Axes of the slice: x: 4, y: 4, z: 4 (z_hi: 2, z_lo: 2; z = z_hi * 2 + z_lo), core: 2. Of those that a mesh axis runs over, the one named last changes fastest.
Arguments:
- tokens: bfloat16 [49152, 8192], P(('fsdp', 'dp')), may hold values from -6 to 6
- output_gradient: bfloat16 [49152, 1024], P(('fsdp', 'dp')), may hold values from -6 to 6
- frozen_value_weight: bfloat16 [8192, 1024], P('fsdp'), may hold values from -0.0625 to 0.0625
- adapter_down_maps: bfloat16 [128, 16, 8192], P(('fsdp', 'dp')), may hold values from -0.0625 to 0.0625
- adapter_up_maps: bfloat16 [128, 16, 1024], P(('fsdp', 'dp')), may hold values from -1.5 to 1.5
- block_tenant_ids: int32 [384], P(('fsdp', 'dp')), may hold values from 0 to 127, as said below
- block_live_rows: int32 [384], P(('fsdp', 'dp')), may hold values from 33 to 128, as said below
- tenant_owner_slot: int32 [128], replicated, may hold values from 0 to 127, as said below
Outputs:
- output: bfloat16 [49152, 1024], P(('fsdp', 'dp'))
- token_gradient: bfloat16 [49152, 8192], P(('fsdp', 'dp'))
- grad_down: bfloat16 [128, 16, 8192], P(('fsdp', 'dp'))
- grad_up: bfloat16 [128, 16, 1024], P(('fsdp', 'dp'))
The draws below stay inside these ranges and needn't reach their ends.
Inputs may be any that keep to these rules, and one draw needn't show every extreme that they name: `block_tenant_ids`: A block held by a device whose index along dp is d names a tenant t with tenant_owner_slot[t] mod (size of dp) = d; tenant_owner_slot is a permutation. `block_live_rows`: the first block of every device is full. `tenant_owner_slot`: each slot is named once.
All inputs are finite; a program needn't handle non-finite values.
Results may differ from the reference program's by a relative error of at most 0.01.
Values may be sent and summed in bfloat16 or wider, within the bound.
A program may use at most 192 MiB of HBM per device.

```python
import jax
import jax.numpy as jnp
from jax import lax

MODEL_DIM = 8192
VALUE_DIM = 1024
ADAPTER_RANK = 16
BLOCK = 128
BLK_DEV = 3
GROUPS = 4
GROUP_ADP = 32
ADAPTER_COUNT = 128
NBLOCKS = 384
TOKENS = 49152
N_FSDP = 32
N_DP = 4


def owner_permutation(key):
    return jax.random.permutation(jax.random.fold_in(key, 7), ADAPTER_COUNT).astype(jnp.int32)


def draw_tenant_owner_slot(key, part):
    return owner_permutation(key)


def draw_block_tenant_ids(key, part):
    perm_table = owner_permutation(key)
    inverse_table = jnp.argsort(perm_table).astype(jnp.int32)
    block_index = jnp.arange(NBLOCKS, dtype=jnp.int32)
    group_index = block_index // BLK_DEV % GROUPS
    member_pick = jax.random.randint(jax.random.fold_in(key, 11), (NBLOCKS,), 0, GROUP_ADP).astype(jnp.int32)
    slot_pick = group_index + GROUPS * member_pick
    return inverse_table[slot_pick].astype(jnp.int32)


def draw_block_live_rows(key, part):
    block_index = jnp.arange(NBLOCKS, dtype=jnp.int32)
    row_pick = jax.random.randint(jax.random.fold_in(key, 13), (NBLOCKS,), BLOCK // 4 + 1, BLOCK + 1).astype(jnp.int32)
    return jnp.where(block_index % BLK_DEV == 0, BLOCK, row_pick).astype(jnp.int32)


def shard_levels(own_key, dims, pieces, least, largest):
    gain, own = 1.0, jax.random.fold_in(own_key, 6)
    for axis_at, blocks in pieces:
        draws = jnp.exp(jax.random.uniform(jax.random.fold_in(own, axis_at), (blocks,), jnp.float32, least / len(pieces), largest / len(pieces)))
        gain = gain * jnp.repeat(draws, dims[axis_at] // blocks).reshape([-1 if axis == axis_at else 1 for axis in range(len(dims))])
    return gain


def gaussian(rng, shape, spread, reach, split=(), kind=jnp.bfloat16):
    entries = spread * jax.random.normal(rng, shape, jnp.float32)
    if split:
        entries = entries * shard_levels(rng, shape, split, -0.22, 0.18)
    return jnp.clip(entries, -reach, reach).astype(kind)


def setup_inputs(seed: int = 0) -> dict:
    arg_keys = jax.random.split(jax.random.key(seed), 9)
    tokens = gaussian(arg_keys[0], (TOKENS, MODEL_DIM), 1.0, 6.0, ((0, 128),))
    output_gradient = gaussian(arg_keys[1], (TOKENS, VALUE_DIM), 1.0, 6.0, ((0, 128),))
    frozen_value_weight = gaussian(arg_keys[2], (MODEL_DIM, VALUE_DIM), MODEL_DIM ** -0.5, 0.0625, ((0, 32),))
    adapter_down_maps = gaussian(arg_keys[3], (ADAPTER_COUNT, ADAPTER_RANK, MODEL_DIM), MODEL_DIM ** -0.5, 0.0625, ((0, 128),))
    adapter_up_maps = gaussian(arg_keys[4], (ADAPTER_COUNT, ADAPTER_RANK, VALUE_DIM), ADAPTER_RANK ** -0.5, 1.5, ((0, 128),))
    block_tenant_ids = draw_block_tenant_ids(jax.random.fold_in(arg_keys[8], 71), 0)
    block_live_rows = draw_block_live_rows(jax.random.fold_in(arg_keys[8], 71), 0)
    tenant_owner_slot = draw_tenant_owner_slot(jax.random.fold_in(arg_keys[8], 71), 0)
    return dict(tokens=tokens, output_gradient=output_gradient, frozen_value_weight=frozen_value_weight, adapter_down_maps=adapter_down_maps, adapter_up_maps=adapter_up_maps, block_tenant_ids=block_tenant_ids, block_live_rows=block_live_rows, tenant_owner_slot=tenant_owner_slot)


ADAPTER_SCALE = 2.0


def reference(tokens, output_gradient, frozen_value_weight, adapter_down_maps, adapter_up_maps, block_tenant_ids, block_live_rows, tenant_owner_slot):
    slot_ids = tenant_owner_slot[block_tenant_ids].astype(jnp.int32)
    live_rows = (jnp.arange(BLOCK)[None, :] < block_live_rows[:, None]).astype(jnp.float32)
    token_blocks = tokens.reshape(NBLOCKS, BLOCK, MODEL_DIM)
    cot_blocks = output_gradient.reshape(NBLOCKS, BLOCK, VALUE_DIM)

    def per_block(items):
        rows_in, cotangent_input, single_slot, mask_one = items
        down_matrix = adapter_down_maps[single_slot]
        up_matrix = adapter_up_maps[single_slot]
        mask_column = mask_one[:, None]
        low_rank_state = (jnp.dot(rows_in, down_matrix.T, preferred_element_type=jnp.float32) * mask_column).astype(jnp.bfloat16)
        low_rank_gradient = (ADAPTER_SCALE * jnp.dot(cotangent_input, up_matrix.T, preferred_element_type=jnp.float32) * mask_column).astype(jnp.bfloat16)
        frozen_output = jnp.dot(rows_in, frozen_value_weight, preferred_element_type=jnp.float32)
        adapter_output = jnp.dot(low_rank_state, up_matrix, preferred_element_type=jnp.float32)
        output_block = (mask_column * (frozen_output + ADAPTER_SCALE * adapter_output)).astype(jnp.bfloat16)
        frozen_backward = jnp.dot(cotangent_input, frozen_value_weight.T, preferred_element_type=jnp.float32)
        adapter_backward = jnp.dot(low_rank_gradient, down_matrix, preferred_element_type=jnp.float32)
        backward_block = (mask_column * (frozen_backward + adapter_backward)).astype(jnp.bfloat16)
        partial_down = jnp.dot(low_rank_gradient.T, rows_in, preferred_element_type=jnp.float32)
        partial_up = ADAPTER_SCALE * jnp.dot(low_rank_state.T, cotangent_input, preferred_element_type=jnp.float32)
        return output_block, backward_block, partial_down, partial_up

    out_blocks, back_blocks, partial_down, partial_up = lax.map(per_block, (token_blocks, cot_blocks, slot_ids, live_rows))
    output = out_blocks.reshape(TOKENS, VALUE_DIM)
    token_gradient = back_blocks.reshape(TOKENS, MODEL_DIM)
    devices_all = N_FSDP * N_DP
    slots_dev = slot_ids.reshape(devices_all, BLK_DEV)
    down_dev = partial_down.reshape(devices_all, BLK_DEV, ADAPTER_RANK * MODEL_DIM)
    up_dev = partial_up.reshape(devices_all, BLK_DEV, ADAPTER_RANK * VALUE_DIM)

    def add_device(totals, items):
        slots_one, down_one, up_one = items
        onehot = (slots_one[:, None] == jnp.arange(ADAPTER_COUNT)[None, :]).astype(jnp.float32)
        term_down = jnp.dot(onehot.T, down_one, precision=lax.Precision.HIGHEST).astype(jnp.bfloat16)
        term_up = jnp.dot(onehot.T, up_one, precision=lax.Precision.HIGHEST).astype(jnp.bfloat16)
        return (totals[0] + term_down.astype(jnp.float32), totals[1] + term_up.astype(jnp.float32)), None

    start_sums = (jnp.zeros((ADAPTER_COUNT, ADAPTER_RANK * MODEL_DIM), jnp.float32), jnp.zeros((ADAPTER_COUNT, ADAPTER_RANK * VALUE_DIM), jnp.float32))
    sums_all, unused = lax.scan(add_device, start_sums, (slots_dev, down_dev, up_dev))
    grad_down = sums_all[0].reshape(ADAPTER_COUNT, ADAPTER_RANK, MODEL_DIM).astype(jnp.bfloat16)
    grad_up = sums_all[1].reshape(ADAPTER_COUNT, ADAPTER_RANK, VALUE_DIM).astype(jnp.bfloat16)
    return (output, token_gradient, grad_down, grad_up)
```

```python
import jax
import jax.numpy as jnp
from jax import lax
from jax.experimental import pallas as pl
from jax.experimental.pallas import tpu as pltpu
from jax.sharding import PartitionSpec as P

ADAPTER_SCALE = 2.0
MESH = pl.DeviceIdType.MESH
F32 = jnp.float32
BF16 = jnp.bfloat16
STEP = 1024
NSEM = 96


def mult(index, of):
    return pl.multiple_of(index, of)


def kernel(
    tok_h, cot_h, w_h, down_h, up_h, ids_s, live_s, owner_v,
    out_h, tg_h, gd_h, gu_h,
    tok, cot, wbuf, src, sel, r1, r2, fin, part, tab, t1, t2, t3, zs, gout,
    acc, xb, db, tgb, outb, meta, smat, lg, low, ls, ts, ss, rs,
):
    rows, model = tok_h.shape
    value = cot_h.shape[1]
    rank = down_h.shape[1]
    nblk = ids_s.shape[0]
    block = rows // nblk
    width = model + value
    picks = nblk * rank
    half = w_h.shape[0] // 2

    f_me = lax.axis_index("fsdp")
    d_me = lax.axis_index("dp")
    zl = f_me // 16
    x = f_me // 4 % 4
    y = f_me % 4
    zh = d_me // 2
    c = d_me % 2
    p = y * (1 - c) + x * c
    q = x * (1 - c) + y * c
    sp = 1 + 3 * c
    sq = 4 - 3 * c
    p_r, p_l, p_o = (p + 1) % 4, (p + 3) % 4, (p + 2) % 4

    def device(zl_, p_, q_):
        return (zl_ * 16 + p_ * sp + q_ * sq, d_me)

    to_z = device(1 - zl, p, q)
    to_pr, to_pl = device(zl, p_r, q), device(zl, p_l, q)
    to_qr, to_ql = device(zl, p, (q + 1) % 4), device(zl, p, (q + 3) % 4)
    to_qo = device(zl, p, (q + 2) % 4)
    to_c = (f_me, zh * 2 + 1 - c)

    count = [0]

    def remote(source, target, where):
        i = count[0]
        count[0] += 1
        return pltpu.make_async_remote_copy(
            src_ref=source, dst_ref=target, send_sem=ss.at[i], recv_sem=rs.at[i],
            device_id=where, device_id_type=MESH,
        )

    def start(copies):
        for copy in copies:
            copy.start()

    def recv(copies):
        for copy in copies:
            copy.wait_recv()

    lc_up = pltpu.make_async_copy(up_h.at[0], src.at[zl, p, :, pl.ds(0, value)], ls.at[0])
    lc_down = pltpu.make_async_copy(down_h.at[0], src.at[zl, p, :, pl.ds(value, model)], ls.at[1])
    lc_cot = pltpu.make_async_copy(cot_h, cot, ls.at[2])
    lc_tok = pltpu.make_async_copy(tok_h, tok, ls.at[3])
    w_own = w_h.at[pl.ds(mult(c * half, half), half)]
    lc_w = pltpu.make_async_copy(w_own, wbuf.at[0, 0, zl * 4 + p], ls.at[4])
    start([lc_up, lc_cot, lc_down, lc_w, lc_tok])

    lane = lax.broadcasted_iota(jnp.int32, (8, 128), 1)
    subl = lax.broadcasted_iota(jnp.int32, (8, 128), 0)
    owners = owner_v[...].astype(F32)
    lane1 = lax.broadcasted_iota(jnp.int32, (1, 128), 1)
    mrow = jnp.zeros((8, 128), F32)
    for b in range(nblk):
        slot = jnp.sum(jnp.where(lane1 == ids_s[b], owners, 0.0), axis=1, keepdims=True)
        mrow = jnp.where(subl == b, slot, mrow)
    meta[0] = mrow

    barrier = pltpu.get_barrier_semaphore()
    partners = (to_z, to_pr, to_pl, to_qr, to_ql, to_qo, to_c)
    for where in partners:
        pl.semaphore_signal(barrier, inc=1, device_id=where, device_id_type=MESH)
    pl.semaphore_wait(barrier, len(partners))

    def gather(own, at):
        z = [remote(own, at(zl, p), to_z)]
        p1o = [remote(own, at(zl, p), to_pr), remote(own, at(zl, p), to_pl)]
        theirs = at(1 - zl, p)
        p1z = [remote(theirs, theirs, to_pr), remote(theirs, theirs, to_pl)]
        p2 = [
            remote(at(0, p_l), at(0, p_l), to_pr),
            remote(at(1, p_r), at(1, p_r), to_pl),
        ]
        return z, p1o, p1z, p2

    def adapter_at(first, size):
        return lambda zl_, p_: src.at[zl_, p_, :, pl.ds(first, size)]

    u_z, u_p1o, u_p1z, u_p2 = gather(up_h.at[0], adapter_at(0, value))
    d_z, d_p1o, d_p1z, d_p2 = gather(down_h.at[0], adapter_at(value, model))
    w_z, w_p1o, w_p1z, w_p2 = gather(w_own, lambda zl_, p_: wbuf.at[0, 0, zl_ * 4 + p_])
    m_q = [
        remote(meta.at[0], meta.at[3], to_qr),
        remote(meta.at[0], meta.at[1], to_ql),
        remote(meta.at[0], meta.at[2], to_qo),
    ]

    def scatter_q(first, size):
        h = size // 2
        h0 = first // 2
        q1 = [
            remote(sel.at[2, :, pl.ds(first, h)], r1.at[0, :, pl.ds(h0, h)], to_qr),
            remote(sel.at[2, :, pl.ds(first + h, h)], r1.at[1, :, pl.ds(h0, h)], to_ql),
        ]
        whole = pl.ds(first, size)
        q2 = [
            remote(sel.at[1, :, whole], r2.at[0, :, whole], to_qr),
            remote(sel.at[3, :, whole], r2.at[1, :, whole], to_ql),
        ]
        return q1, q2

    u_q1, u_q2 = scatter_q(0, value)
    d_q1, d_q2 = scatter_q(value, model)

    def grads(first, size):
        h = size // 2
        whole = pl.ds(first, size)
        q1 = [
            remote(part.at[0, :, whole], part.at[3, :, whole], to_qr),
            remote(part.at[0, :, whole], part.at[1, :, whole], to_ql),
        ]
        lo, hi = pl.ds(first, h), pl.ds(first + h, h)
        q2 = [
            remote(part.at[3, :, lo], part.at[2, :, lo], to_qr),
            remote(part.at[1, :, hi], part.at[2, :, hi], to_ql),
        ]
        p1 = [
            remote(tab.at[0, p_o, :, whole], t1.at[0, :, whole], to_pr),
            remote(tab.at[1, p_o, :, whole], t1.at[1, :, whole], to_pl),
        ]
        p2 = [
            remote(tab.at[:, p_r, :, whole], t2.at[0, :, :, whole], to_pr),
            remote(tab.at[:, p_l, :, whole], t2.at[1, :, :, whole], to_pl),
        ]
        z = [remote(zs.at[:, whole], t3.at[:, whole], to_z)]
        return q1, q2, p1, p2, z

    gd = grads(value, model)
    gu = grads(0, value)

    def w_part(dq, zl_):
        return wbuf.at[0, dq, pl.ds(zl_ * 4, 4)]

    w_q1 = [
        remote(w_part(0, 0), w_part(3, 0), to_qr),
        remote(w_part(0, 1), w_part(1, 1), to_ql),
        remote(w_part(0, 1), w_part(3, 1), to_qr),
        remote(w_part(0, 0), w_part(1, 0), to_ql),
    ]
    w_q2 = [
        remote(w_part(3, 0), w_part(2, 0), to_qr),
        remote(w_part(1, 1), w_part(2, 1), to_ql),
    ]
    w_c = [remote(wbuf.at[0, dq], wbuf.at[1, dq], to_c) for dq in range(4)]

    start(u_z + u_p1o + m_q + d_z + d_p1o + w_z + w_p1o)

    def columns(first, j, step=STEP):
        return pl.ds(mult(first + j * step, 128), step)

    def loop(size, body, step=STEP):
        if size <= step:
            body(0, size)
        else:
            def run(j, carry):
                body(j, step)
                return carry
            lax.fori_loop(0, size // step, run, 0)

    def build_selection():
        lanes = lax.broadcasted_iota(jnp.int32, (1, 128), 1)
        j = lanes // 16
        target = (((j // 4) * 16 + (j % 4) * sp + q * sq) * 4 + d_me).astype(F32)
        same = lax.broadcasted_iota(jnp.int32, (16, 128), 0) == (
            lax.broadcasted_iota(jnp.int32, (16, 128), 1) % 16
        )
        for dq in range(4):
            for b in range(nblk):
                hit = jnp.logical_and(same, meta[dq, b : b + 1, :] == target)
                r0 = (dq * nblk + b) * rank
                smat[r0 : r0 + rank, :] = jnp.where(hit, 1.0, 0.0).astype(BF16)

    def select(first, size):
        def one(j, step):
            cols = columns(first, j, step)
            held = src[:, :, :, cols].reshape(8 * rank, step)
            picked = jnp.dot(smat[...], held, preferred_element_type=F32)
            sel[:, :, cols] = picked.astype(BF16).reshape(4, picks, step)
        loop(size, one)

    def add_halves(first, size):
        h = size // 2
        h0 = first // 2

        def one(j, step):
            from_l, from_r = columns(first, j, step), columns(first + h, j, step)
            got = columns(h0, j, step)
            sel[1, :, from_l] = sel[1, :, from_l] + r1[0, :, got]
            sel[3, :, from_r] = sel[3, :, from_r] + r1[1, :, got]
        loop(h, one)

    def finish_selection(first, size):
        def one(j, step):
            cols = columns(first, j, step)
            fin[:, cols] = sel[0, :, cols] + r2[0, :, cols] + r2[1, :, cols]
        loop(size, one)

    def build_table(first, size):
        def one(j, step):
            cols = columns(first, j, step)
            held = part[:, :, cols].reshape(4 * picks, step)
            total = lax.dot_general(
                smat[...], held, (((0,), (0,)), ((), ())), preferred_element_type=F32
            )
            tab[:, :, :, cols] = total.astype(BF16).reshape(2, 4, rank, step)
        loop(size, one)

    def add_table(first, size):
        def one(j, step):
            cols = columns(first, j, step)
            a = tab[0, p_r, :, cols].astype(F32) + t1[0, :, cols].astype(F32)
            tab[0, p_r, :, cols] = a.astype(BF16)
            a = tab[1, p_l, :, cols].astype(F32) + t1[1, :, cols].astype(F32)
            tab[1, p_l, :, cols] = a.astype(BF16)
        loop(size, one)

    def sum_three(zl_, cols):
        return (
            tab[zl_, p, :, cols].astype(F32)
            + t2[0, zl_, :, cols].astype(F32)
            + t2[1, zl_, :, cols].astype(F32)
        )

    def send_table(first, size):
        def one(j, step):
            cols = columns(first, j, step)
            zs[:, cols] = sum_three(1 - zl, cols).astype(BF16)
        loop(size, one)

    def finish_table(first, size):
        def one(j, step):
            cols = columns(first, j, step)
            gout[:, cols] = (sum_three(zl, cols) + t3[:, cols].astype(F32)).astype(BF16)
        loop(size, one)

    def live_mask(shape):
        r = lax.broadcasted_iota(jnp.int32, shape, 0)
        limit = jnp.zeros(shape, jnp.int32)
        for b in range(nblk):
            limit = jnp.where(r // block == b, live_s[b] + b * block, limit)
        return r < limit

    def block_mask():
        r = lax.broadcasted_iota(jnp.int32, (rows, picks), 0)
        k = lax.broadcasted_iota(jnp.int32, (rows, picks), 1)
        return jnp.logical_and(r // block == k // rank, live_mask((rows, picks)))

    def batch(g, dq, t, wait):
        spg = sp + g * (sq - sp)
        sqg = sq + g * (sp - sq)
        qg = q + g * (p - q)
        hg = c + g * (1 - 2 * c)
        slot = t % 2

        def place(i):
            f = (i // 4) * 16 + (i % 4) * spg + ((qg + dq) % 4) * sqg
            return mult(f * (2 * half) + hg * half, half)

        def take(i, carry):
            at = pl.ds(mult(i * half, half), half)
            xb[:, at] = tok[:, pl.ds(place(i), half)]
            db[:, at] = fin[:, pl.ds(mult(value + place(i), half), half)]
            return carry
        lax.fori_loop(0, 8, take, 0)

        def forward(n, carry):
            cols = pl.ds(mult(n * 256, 256), 256)
            w = wbuf[g, dq, :, :, cols].reshape(8 * half, 256)
            acc[:, cols] += jnp.dot(xb[...], w, preferred_element_type=F32)
            return carry
        lax.fori_loop(0, value // 256, forward, 0)

        def out_copy(i):
            return pltpu.make_async_copy(
                tgb.at[slot, :, pl.ds(mult(i * half, half), half)],
                tg_h.at[:, pl.ds(place(i), half)],
                ts.at[slot, i],
            )

        if wait:
            def settle(i, carry):
                out_copy(i).wait()
                return carry
            lax.fori_loop(0, 8, settle, 0)

        def backward(m, carry):
            w = wbuf[g, dq, pl.ds(m * 2, 2), :, :].reshape(2 * half, value)
            at = pl.ds(mult(m * 2 * half, 2 * half), 2 * half)
            got = lax.dot_general(
                cot[...], w, (((1,), (1,)), ((), ())), preferred_element_type=F32
            )
            got = got + jnp.dot(lg[...], db[:, at], preferred_element_type=F32)
            tgb[slot, :, at] = got.astype(BF16)
            return carry
        lax.fori_loop(0, 4, backward, 0)

        def send_out(i, carry):
            out_copy(i).start()
            return carry
        lax.fori_loop(0, 8, send_out, 0)

    U = (0, value)
    D = (value, model)

    recv(u_z)
    start(u_p1z)
    recv(u_p1o + u_p1z)
    start(u_p2)
    recv(d_z)
    start(d_p1z)
    recv(m_q)
    build_selection()
    lc_up.wait()
    recv(u_p2)
    select(*U)
    start(u_q1)
    recv(w_z)
    start(w_p1z)
    recv(u_q1)
    add_halves(*U)
    start(u_q2)
    recv(d_p1o + d_p1z)
    start(d_p2)
    lc_cot.wait()
    cot[...] = jnp.where(live_mask((rows, value)), cot[...].astype(F32), 0.0).astype(BF16)
    recv(u_q2)
    finish_selection(*U)

    back = lax.dot_general(
        cot[...], fin[:, pl.ds(0, value)], (((1,), (1,)), ((), ())), preferred_element_type=F32
    )
    lg[...] = jnp.where(block_mask(), ADAPTER_SCALE * back, 0.0).astype(BF16)
    lc_tok.wait()

    def down_part(j, step):
        got = lax.dot_general(
            lg[...], tok[:, columns(0, j, step)], (((0,), (0,)), ((), ())),
            preferred_element_type=F32,
        )
        part[0, :, columns(value, j, step)] = got.astype(BF16)
    loop(model, down_part)
    start(gd[0])

    lc_down.wait()
    recv(d_p2)
    select(*D)
    start(d_q1)
    recv(w_p1o + w_p1z)
    start(w_p2)
    lc_w.wait()
    recv(w_p2)
    start(w_q1)
    start([w_c[0]])
    recv(gd[0])
    start(gd[1])
    recv(d_q1)
    add_halves(*D)
    start(d_q2)
    recv(gd[1])
    build_table(*D)
    start(gd[2])
    recv(d_q2)
    finish_selection(*D)

    def low_part(j, total):
        return total + lax.dot_general(
            tok[:, columns(0, j)], fin[:, columns(value, j)], (((1,), (1,)), ((), ())),
            preferred_element_type=F32,
        )
    total = lax.fori_loop(0, model // STEP, low_part, jnp.zeros((rows, picks), F32))
    low[...] = jnp.where(block_mask(), total, 0.0).astype(BF16)
    up_part = lax.dot_general(
        low[...], cot[...], (((0,), (0,)), ((), ())), preferred_element_type=F32
    )
    part[0, :, pl.ds(0, value)] = (ADAPTER_SCALE * up_part).astype(BF16)
    start(gu[0])
    acc[...] = ADAPTER_SCALE * jnp.dot(
        low[...], fin[:, pl.ds(0, value)], preferred_element_type=F32
    )
    recv(gd[2])
    add_table(*D)
    start(gd[3])
    recv(gu[0])
    start(gu[1])
    recv([w_c[0]])

    def first_batches(i, carry):
        batch(i, 0, i, False)
        return carry
    lax.fori_loop(0, 2, first_batches, 0)
    recv(gd[3])
    send_table(*D)
    start(gd[4])
    recv(gu[1])
    build_table(*U)
    start(gu[2])
    recv([w_q1[0], w_q1[1]])
    start(w_q2)
    recv(gu[2])
    add_table(*U)
    start(gu[3])
    recv([w_q1[2], w_q1[3]])
    start([w_c[1], w_c[3]])
    recv(gd[4])
    finish_table(*D)
    o_gd = pltpu.make_async_copy(gout.at[:, pl.ds(value, model)], gd_h.at[0], ls.at[5])
    o_gd.start()
    recv(gu[3])
    send_table(*U)
    start(gu[4])
    recv([w_c[1], w_c[3]])

    def middle_batches(i, carry):
        batch(i // 2, 1 + 2 * (i % 2), i + 2, True)
        return carry
    lax.fori_loop(0, 4, middle_batches, 0)
    recv(gu[4])
    finish_table(*U)
    o_gu = pltpu.make_async_copy(gout.at[:, pl.ds(0, value)], gu_h.at[0], ls.at[6])
    o_gu.start()
    recv(w_q2)
    start([w_c[2]])
    recv([w_c[2]])

    def last_batches(i, carry):
        batch(i, 2, i + 6, True)
        return carry
    lax.fori_loop(0, 2, last_batches, 0)
    outb[...] = jnp.where(live_mask((rows, value)), acc[...], 0.0).astype(BF16)
    o_out = pltpu.make_async_copy(outb, out_h, ls.at[7])
    o_out.start()

    sent = u_z + u_p1o + u_p1z + u_p2 + d_z + d_p1o + d_p1z + d_p2 + w_z + w_p1o + w_p1z + w_p2
    sent = sent + m_q + u_q1 + u_q2 + d_q1 + d_q2 + w_q1 + w_q2 + w_c
    for group in gd + gu:
        sent = sent + group
    for copy in sent:
        copy.wait_send()
    o_gd.wait()
    o_gu.wait()
    o_out.wait()
    for slot in range(2):
        for i in range(8):
            pltpu.make_async_copy(
                tgb.at[slot, :, pl.ds(i * half, half)],
                tg_h.at[:, pl.ds(i * half, half)],
                ts.at[slot, i],
            ).wait()


def on_device(
    tokens,
    output_gradient,
    frozen_value_weight,
    adapter_down_maps,
    adapter_up_maps,
    block_tenant_ids,
    block_live_rows,
    tenant_owner_slot,
):
    rows, model = tokens.shape
    value = output_gradient.shape[1]
    rank = adapter_down_maps.shape[1]
    nblk = block_tenant_ids.shape[0]
    picks = nblk * rank
    width = model + value
    half = frozen_value_weight.shape[0] // 2
    hbm = pl.BlockSpec(memory_space=pl.ANY)
    smem = pl.BlockSpec(memory_space=pltpu.SMEM)
    vmem = pl.BlockSpec(memory_space=pltpu.VMEM)
    flops = 4 * rows * model * value
    return pl.pallas_call(
        kernel,
        out_shape=(
            jax.ShapeDtypeStruct((rows, value), BF16),
            jax.ShapeDtypeStruct((rows, model), BF16),
            jax.ShapeDtypeStruct((1, rank, model), BF16),
            jax.ShapeDtypeStruct((1, rank, value), BF16),
        ),
        in_specs=[hbm] * 5 + [smem, smem, vmem],
        out_specs=(hbm, hbm, hbm, hbm),
        scratch_shapes=[
            pltpu.VMEM((rows, model), BF16),
            pltpu.VMEM((rows, value), BF16),
            pltpu.VMEM((2, 4, 8, half, value), BF16),
            pltpu.VMEM((2, 4, rank, width), BF16),
            pltpu.VMEM((4, picks, width), BF16),
            pltpu.VMEM((2, picks, width // 2), BF16),
            pltpu.VMEM((2, picks, width), BF16),
            pltpu.VMEM((picks, width), BF16),
            pltpu.VMEM((4, picks, width), BF16),
            pltpu.VMEM((2, 4, rank, width), BF16),
            pltpu.VMEM((2, rank, width), BF16),
            pltpu.VMEM((2, 2, rank, width), BF16),
            pltpu.VMEM((rank, width), BF16),
            pltpu.VMEM((rank, width), BF16),
            pltpu.VMEM((rank, width), BF16),
            pltpu.VMEM((rows, value), F32),
            pltpu.VMEM((rows, 8 * half), BF16),
            pltpu.VMEM((picks, 8 * half), BF16),
            pltpu.VMEM((2, rows, 8 * half), BF16),
            pltpu.VMEM((rows, value), BF16),
            pltpu.VMEM((4, 8, 128), F32),
            pltpu.VMEM((4 * picks, 8 * rank), BF16),
            pltpu.VMEM((rows, picks), BF16),
            pltpu.VMEM((rows, picks), BF16),
            pltpu.SemaphoreType.DMA((8,)),
            pltpu.SemaphoreType.DMA((2, 8)),
            pltpu.SemaphoreType.DMA((NSEM,)),
            pltpu.SemaphoreType.DMA((NSEM,)),
        ],
        compiler_params=pltpu.CompilerParams(
            collective_id=0, has_side_effects=True, vmem_limit_bytes=58 * 2**20
        ),
        cost_estimate=pl.CostEstimate(
            flops=flops, bytes_accessed=4 * rows * model, transcendentals=0
        ),
    )(
        tokens,
        output_gradient,
        frozen_value_weight,
        adapter_down_maps,
        adapter_up_maps,
        block_tenant_ids,
        block_live_rows,
        tenant_owner_slot.reshape(1, -1),
    )


def solution(mesh):
    placed = (
        P(("fsdp", "dp"), None),
        P(("fsdp", "dp"), None),
        P("fsdp", None),
        P(("fsdp", "dp"), None, None),
        P(("fsdp", "dp"), None, None),
        P(("fsdp", "dp")),
        P(("fsdp", "dp")),
        P(),
    )
    return jax.shard_map(
        on_device,
        mesh=mesh,
        in_specs=placed,
        out_specs=(
            P(("fsdp", "dp"), None),
            P(("fsdp", "dp"), None),
            P(("fsdp", "dp"), None, None),
            P(("fsdp", "dp"), None, None),
        ),
        check_vma=False,
    )
```

```python
import jax
import jax.numpy as jnp
from jax import lax
from jax.experimental import pallas as pl
from jax.experimental.pallas import tpu as pltpu
from jax.sharding import PartitionSpec as P

ADAPTER_SCALE = 2.0
MESH = pl.DeviceIdType.MESH
F32 = jnp.float32
BF16 = jnp.bfloat16
STEP = 1024
NSEM = 128
PARTS = 2
ORDER = (
    "U S D0 D1", "W W M U", "D0 W D1 U", "W D0 D1 S", "U W W D0", "D1 U C W",
    "W W D0 D1", "U LG G0 G1", "D0 D1 L G0", "GU L C B", "W W B G1", "B G0 GU G1",
    "B G0 GU G1", "B C B G0", "GU B G1 GU", "B G0 G1 GU",
)


def mult(index, of):
    return pl.multiple_of(index, of)


def kernel(
    tok_h, cot_h, w_h, down_h, up_h, ids_s, live_s, owner_v,
    out_h, tg_h, gd_h, gu_h,
    tok, cot, wbuf, src, sel, r1, r2, fin, part, tab, t1, t2, t3, zs, gout,
    acc, xb, db, tgb, outb, meta, smat, lg, low, ls, ts, ss, rs,
):
    rows, model = tok_h.shape
    value = cot_h.shape[1]
    rank = down_h.shape[1]
    nblk = ids_s.shape[0]
    block = rows // nblk
    width = model + value
    picks = nblk * rank
    half = w_h.shape[0] // 2

    f_me = lax.axis_index("fsdp")
    d_me = lax.axis_index("dp")
    zl = f_me // 16
    x = f_me // 4 % 4
    y = f_me % 4
    zh = d_me // 2
    c = d_me % 2
    p = y * (1 - c) + x * c
    q = x * (1 - c) + y * c
    sp = 1 + 3 * c
    sq = 4 - 3 * c
    p_r, p_l, p_o = (p + 1) % 4, (p + 3) % 4, (p + 2) % 4

    def device(zl_, p_, q_):
        return (zl_ * 16 + p_ * sp + q_ * sq, d_me)

    to_z = device(1 - zl, p, q)
    z = zh * 2 + zl

    def along_z(z_):
        return (z_ % 2 * 16 + f_me % 16, z_ // 2 * 2 + c)

    to_zu, to_zd = along_z((z + 1) % 4), along_z((z + 3) % 4)
    to_pr, to_pl = device(zl, p_r, q), device(zl, p_l, q)
    to_qr, to_ql = device(zl, p, (q + 1) % 4), device(zl, p, (q + 3) % 4)
    to_qo = device(zl, p, (q + 2) % 4)
    to_c = (f_me, zh * 2 + 1 - c)

    count = [0]

    def remote(source, target, where):
        i = count[0]
        count[0] += 1
        return pltpu.make_async_remote_copy(
            src_ref=source, dst_ref=target, send_sem=ss.at[i], recv_sem=rs.at[i],
            device_id=where, device_id_type=MESH,
        )

    def start(copies):
        for copy in copies:
            copy.start()

    def recv(copies):
        for copy in copies:
            copy.wait_recv()

    lc_up = pltpu.make_async_copy(up_h.at[0], src.at[zl, p, :, pl.ds(0, value)], ls.at[0])
    lc_down = pltpu.make_async_copy(down_h.at[0], src.at[zl, p, :, pl.ds(value, model)], ls.at[1])
    lc_cot = pltpu.make_async_copy(cot_h, cot, ls.at[2])
    lc_tok = pltpu.make_async_copy(tok_h, tok, ls.at[3])
    w_own = w_h.at[pl.ds(mult(c * half, half), half)]
    lc_w = pltpu.make_async_copy(w_own, wbuf.at[0, 0, zl * 4 + p], ls.at[4])
    start([lc_up, lc_cot, lc_down, lc_w, lc_tok])

    lane = lax.broadcasted_iota(jnp.int32, (8, 128), 1)
    subl = lax.broadcasted_iota(jnp.int32, (8, 128), 0)
    owners = owner_v[...].astype(F32)
    lane1 = lax.broadcasted_iota(jnp.int32, (1, 128), 1)
    mrow = jnp.zeros((8, 128), F32)
    for b in range(nblk):
        slot = jnp.sum(jnp.where(lane1 == ids_s[b], owners, 0.0), axis=1, keepdims=True)
        mrow = jnp.where(subl == b, slot, mrow)
    meta[0] = mrow

    barrier = pltpu.get_barrier_semaphore()
    partners = (to_zu, to_zd, to_pr, to_pl, to_qr, to_ql, to_qo, to_c)
    for where in partners:
        pl.semaphore_signal(barrier, inc=1, device_id=where, device_id_type=MESH)
    pl.semaphore_wait(barrier, len(partners))

    def gather(own, at):
        z = [remote(own, at(zl, p), to_z)]
        p1o = [remote(own, at(zl, p), to_pr), remote(own, at(zl, p), to_pl)]
        theirs = at(1 - zl, p)
        p1z = [remote(theirs, theirs, to_pr), remote(theirs, theirs, to_pl)]
        p2 = [
            remote(at(0, p_l), at(0, p_l), to_pr),
            remote(at(1, p_r), at(1, p_r), to_pl),
        ]
        return z, p1o, p1z, p2

    def adapter_at(first, size):
        return lambda zl_, p_: src.at[zl_, p_, :, pl.ds(first, size)]

    m_q = [
        remote(meta.at[0], meta.at[3], to_qr),
        remote(meta.at[0], meta.at[1], to_ql),
        remote(meta.at[0], meta.at[2], to_qo),
    ]

    def scatter_q(first, size):
        h = size // 2
        h0 = first // 2
        q1 = [
            remote(sel.at[2, :, pl.ds(first, h)], r1.at[0, :, pl.ds(h0, h)], to_qr),
            remote(sel.at[2, :, pl.ds(first + h, h)], r1.at[1, :, pl.ds(h0, h)], to_ql),
        ]
        whole = pl.ds(first, size)
        q2 = [
            remote(sel.at[1, :, whole], r2.at[0, :, whole], to_qr),
            remote(sel.at[3, :, whole], r2.at[1, :, whole], to_ql),
        ]
        return q1, q2

    def grads(first, size):
        h = size // 2
        whole = pl.ds(first, size)
        q1 = [
            remote(part.at[0, :, whole], part.at[3, :, whole], to_qr),
            remote(part.at[0, :, whole], part.at[1, :, whole], to_ql),
        ]
        lo, hi = pl.ds(first, h), pl.ds(first + h, h)
        q2 = [
            remote(part.at[3, :, lo], part.at[2, :, lo], to_qr),
            remote(part.at[1, :, hi], part.at[2, :, hi], to_ql),
        ]
        p1 = [
            remote(tab.at[0, p_o, :, whole], t1.at[0, :, whole], to_pr),
            remote(tab.at[1, p_o, :, whole], t1.at[1, :, whole], to_pl),
        ]
        p2 = [
            remote(tab.at[:, p_r, :, whole], t2.at[0, :, :, whole], to_pr),
            remote(tab.at[:, p_l, :, whole], t2.at[1, :, :, whole], to_pl),
        ]
        z = [remote(zs.at[:, whole], t3.at[:, whole], to_z)]
        return q1, q2, p1, p2, z

    def piece(dq, zl_, p_):
        return wbuf.at[0, dq, zl_ * 4 + p_]

    def rows_of(ref, first, size):
        return ref.at[pl.ds(first, size)]

    order = (p, p_l, p_r, p_o)
    held = [w_own] + [piece(0, zl, k) for k in order[1:]]
    w_p1 = [remote(w_own, piece(0, zl, p), to_pr), remote(w_own, piece(0, zl, p), to_pl)]
    w_p2 = [
        remote(rows_of(held[1], 0, half // 2), rows_of(held[1], 0, half // 2), to_pr),
        remote(rows_of(held[2], half // 2, half // 2), rows_of(held[2], half // 2, half // 2), to_pl),
    ]
    w_q1, w_q2, w_z0, w_z1, w_z2 = [], [], [], [], []
    for j in range(4):
        k = order[j]
        up, down = (to_zu, to_zd) if j % 2 == 0 else (to_zd, to_zu)
        w_q1.append([
            remote(held[j], piece(3, zl, k), to_qr),
            remote(held[j], piece(1, zl, k), to_ql),
        ])
        w_z0.append(remote(held[j], piece(0, zl, k), up))
        w_z1.append([
            remote(piece(3, zl, k), piece(3, zl, k), up),
            remote(piece(1, zl, k), piece(1, zl, k), down),
        ])
        if j < 2:
            w_q2.append(remote(piece(3, zl, k), piece(2, zl, k), to_qr))
        else:
            w_q2.append(remote(piece(1, zl, k), piece(2, zl, k), to_ql))
        w_z2.append(remote(piece(2, zl, k), piece(2, zl, k), up))
    w_c = [remote(wbuf.at[0, dq], wbuf.at[1, dq], to_c) for dq in range(4)]

    sent = []

    def go(copies):
        sent.extend(copies)
        start(copies)

    def columns(first, j, step=STEP):
        return pl.ds(mult(first + j * step, 128), step)

    def loop(size, body, step=STEP):
        if size <= step:
            body(0, size)
        else:
            def run(j, carry):
                body(j, step)
                return carry
            lax.fori_loop(0, size // step, run, 0)

    def build_selection():
        lanes = lax.broadcasted_iota(jnp.int32, (1, 128), 1)
        j = lanes // 16
        target = (((j // 4) * 16 + (j % 4) * sp + q * sq) * 4 + d_me).astype(F32)
        same = lax.broadcasted_iota(jnp.int32, (16, 128), 0) == (
            lax.broadcasted_iota(jnp.int32, (16, 128), 1) % 16
        )
        for dq in range(4):
            for b in range(nblk):
                hit = jnp.logical_and(same, meta[dq, b : b + 1, :] == target)
                r0 = (dq * nblk + b) * rank
                smat[r0 : r0 + rank, :] = jnp.where(hit, 1.0, 0.0).astype(BF16)

    def select(first, size):
        def one(j, step):
            cols = columns(first, j, step)
            held = src[:, :, :, cols].reshape(8 * rank, step)
            picked = jnp.dot(smat[...], held, preferred_element_type=F32)
            sel[:, :, cols] = picked.astype(BF16).reshape(4, picks, step)
        loop(size, one)

    def add_halves(first, size):
        h = size // 2
        h0 = first // 2

        def one(j, step):
            from_l, from_r = columns(first, j, step), columns(first + h, j, step)
            got = columns(h0, j, step)
            sel[1, :, from_l] = sel[1, :, from_l] + r1[0, :, got]
            sel[3, :, from_r] = sel[3, :, from_r] + r1[1, :, got]
        loop(h, one)

    def finish_selection(first, size):
        def one(j, step):
            cols = columns(first, j, step)
            fin[:, cols] = sel[0, :, cols] + r2[0, :, cols] + r2[1, :, cols]
        loop(size, one)

    def build_table(first, size):
        def one(j, step):
            cols = columns(first, j, step)
            held = part[:, :, cols].reshape(4 * picks, step)
            total = lax.dot_general(
                smat[...], held, (((0,), (0,)), ((), ())), preferred_element_type=F32
            )
            tab[:, :, :, cols] = total.astype(BF16).reshape(2, 4, rank, step)
        loop(size, one)

    def add_table(first, size):
        def one(j, step):
            cols = columns(first, j, step)
            a = tab[0, p_r, :, cols].astype(F32) + t1[0, :, cols].astype(F32)
            tab[0, p_r, :, cols] = a.astype(BF16)
            a = tab[1, p_l, :, cols].astype(F32) + t1[1, :, cols].astype(F32)
            tab[1, p_l, :, cols] = a.astype(BF16)
        loop(size, one)

    def sum_three(zl_, cols):
        return (
            tab[zl_, p, :, cols].astype(F32)
            + t2[0, zl_, :, cols].astype(F32)
            + t2[1, zl_, :, cols].astype(F32)
        )

    def send_table(first, size):
        def one(j, step):
            cols = columns(first, j, step)
            zs[:, cols] = sum_three(1 - zl, cols).astype(BF16)
        loop(size, one)

    def finish_table(first, size):
        def one(j, step):
            cols = columns(first, j, step)
            gout[:, cols] = (sum_three(zl, cols) + t3[:, cols].astype(F32)).astype(BF16)
        loop(size, one)

    def live_mask(shape):
        r = lax.broadcasted_iota(jnp.int32, shape, 0)
        limit = jnp.zeros(shape, jnp.int32)
        for b in range(nblk):
            limit = jnp.where(r // block == b, live_s[b] + b * block, limit)
        return r < limit

    def block_mask():
        r = lax.broadcasted_iota(jnp.int32, (rows, picks), 0)
        k = lax.broadcasted_iota(jnp.int32, (rows, picks), 1)
        return jnp.logical_and(r // block == k // rank, live_mask((rows, picks)))

    def batch(g, dq, t, wait):
        spg = sp + g * (sq - sp)
        sqg = sq + g * (sp - sq)
        qg = q + g * (p - q)
        hg = c + g * (1 - 2 * c)
        slot = t % 2

        def place(i):
            f = (i // 4) * 16 + (i % 4) * spg + ((qg + dq) % 4) * sqg
            return mult(f * (2 * half) + hg * half, half)

        def take(i, carry):
            at = pl.ds(mult(i * half, half), half)
            xb[:, at] = tok[:, pl.ds(place(i), half)]
            db[:, at] = fin[:, pl.ds(mult(value + place(i), half), half)]
            return carry
        lax.fori_loop(0, 8, take, 0)

        def forward(n, carry):
            cols = pl.ds(mult(n * 256, 256), 256)
            w = wbuf[g, dq, :, :, cols].reshape(8 * half, 256)
            acc[:, cols] += jnp.dot(xb[...], w, preferred_element_type=F32)
            return carry
        lax.fori_loop(0, value // 256, forward, 0)

        def out_copy(i):
            return pltpu.make_async_copy(
                tgb.at[slot, :, pl.ds(mult(i * half, half), half)],
                tg_h.at[:, pl.ds(place(i), half)],
                ts.at[slot, i],
            )

        if wait:
            def settle(i, carry):
                out_copy(i).wait()
                return carry
            lax.fori_loop(0, 8, settle, 0)

        def backward(m, carry):
            w = wbuf[g, dq, pl.ds(m * 2, 2), :, :].reshape(2 * half, value)
            at = pl.ds(mult(m * 2 * half, 2 * half), 2 * half)
            got = lax.dot_general(
                cot[...], w, (((1,), (1,)), ((), ())), preferred_element_type=F32
            )
            got = got + jnp.dot(lg[...], db[:, at], preferred_element_type=F32)
            tgb[slot, :, at] = got.astype(BF16)
            return carry
        lax.fori_loop(0, 4, backward, 0)

        def send_out(i, carry):
            out_copy(i).start()
            return carry
        lax.fori_loop(0, 8, send_out, 0)

    def adapter_chain(own, first, size):
        z1, p1o, p1z, p2 = gather(own, adapter_at(first, size))
        q1, q2 = scatter_q(first, size)
        go(z1 + p1o)
        yield
        recv(z1)
        go(p1z)
        yield
        recv(p1o + p1z)
        go(p2)
        yield
        recv(p2)
        select(first, size)
        go(q1)
        yield
        recv(q1)
        add_halves(first, size)
        go(q2)
        yield
        recv(q2)
        finish_selection(first, size)
        yield

    def gradient_chain(first, size, make):
        q1, q2, p1, p2, z1 = grads(first, size)
        make()
        go(q1)
        yield
        recv(q1)
        go(q2)
        yield
        recv(q2)
        build_table(first, size)
        go(p1)
        yield
        recv(p1)
        add_table(first, size)
        go(p2)
        yield
        recv(p2)
        send_table(first, size)
        go(z1)
        yield
        recv(z1)
        finish_table(first, size)
        yield

    def weight_chain():
        go(w_p1)
        yield
        go(w_q1[0] + [w_z0[0]])
        yield
        recv([w_p1[0]])
        go([w_p2[0]] + w_q1[1] + [w_z0[1]])
        yield
        recv([w_p1[1]])
        go([w_p2[1]] + w_q1[2] + [w_z0[2]])
        yield
        recv(w_p2)
        go(w_q1[3] + [w_z0[3]])
        yield
        for j in range(4):
            recv(w_q1[j])
            go(w_z1[j] + [w_q2[j]])
            yield
        for j in (0, 2):
            recv(w_q2[j : j + 2])
            go(w_z2[j : j + 2])
            yield

    def core_chain():
        lc_w.wait()
        recv(w_z0)
        go([w_c[0]])
        yield
        for pair in w_z1:
            recv(pair)
        go([w_c[1], w_c[3]])
        yield
        recv(w_z2)
        go([w_c[2]])
        yield

    def batch_chain():
        t = 0
        for g, dq in ((0, 0), (0, 1), (0, 3), (1, 0), (1, 1), (1, 3), (0, 2), (1, 2)):
            if g == 1:
                recv([w_c[dq]])
            batch(g, dq, t, t >= 2)
            t += 1
            yield

    def mask_chain():
        lc_cot.wait()
        cot[...] = jnp.where(live_mask((rows, value)), cot[...].astype(F32), 0.0).astype(BF16)
        lc_up.wait()
        lc_down.wait()
        yield

    def meta_chain():
        go(m_q)
        yield
        recv(m_q)
        build_selection()
        yield

    def low_gradient_chain():
        back = lax.dot_general(
            cot[...], fin[:, pl.ds(0, value)], (((1,), (1,)), ((), ())), preferred_element_type=F32
        )
        lg[...] = jnp.where(block_mask(), ADAPTER_SCALE * back, 0.0).astype(BF16)
        lc_tok.wait()
        yield

    def down_parts(first, size):
        def make():
            def down_part(j, step):
                got = lax.dot_general(
                    lg[...], tok[:, columns(first - value, j, step)], (((0,), (0,)), ((), ())),
                    preferred_element_type=F32,
                )
                part[0, :, columns(first, j, step)] = got.astype(BF16)
            loop(size, down_part)
        return make

    def low_chain():
        def low_part(j, total):
            return total + lax.dot_general(
                tok[:, columns(0, j)], fin[:, columns(value, j)], (((1,), (1,)), ((), ())),
                preferred_element_type=F32,
            )
        total = lax.fori_loop(0, model // STEP, low_part, jnp.zeros((rows, picks), F32))
        low[...] = jnp.where(block_mask(), total, 0.0).astype(BF16)
        yield
        acc[...] = ADAPTER_SCALE * jnp.dot(
            low[...], fin[:, pl.ds(0, value)], preferred_element_type=F32
        )
        yield

    def up_part():
        got = lax.dot_general(
            low[...], cot[...], (((0,), (0,)), ((), ())), preferred_element_type=F32
        )
        part[0, :, pl.ds(0, value)] = (ADAPTER_SCALE * got).astype(BF16)

    chains = {
        "U": adapter_chain(up_h.at[0], 0, value),
        "GU": gradient_chain(0, value, up_part),
        "W": weight_chain(),
        "C": core_chain(),
        "B": batch_chain(),
        "M": mask_chain(),
        "S": meta_chain(),
        "LG": low_gradient_chain(),
        "L": low_chain(),
    }
    size = model // PARTS
    for k in range(PARTS):
        own = down_h.at[0, :, pl.ds(k * size, size)]
        chains["D%d" % k] = adapter_chain(own, value + k * size, size)
        chains["G%d" % k] = gradient_chain(
            value + k * size, size, down_parts(value + k * size, size)
        )
    for name in " ".join(ORDER).split():
        next(chains[name])

    outb[...] = jnp.where(live_mask((rows, value)), acc[...], 0.0).astype(BF16)
    outs = [
        pltpu.make_async_copy(outb, out_h, ls.at[5]),
        pltpu.make_async_copy(gout.at[:, pl.ds(value, model)], gd_h.at[0], ls.at[6]),
        pltpu.make_async_copy(gout.at[:, pl.ds(0, value)], gu_h.at[0], ls.at[7]),
    ]
    start(outs)

    for copy in sent:
        copy.wait_send()
    for copy in outs:
        copy.wait()
    for slot in range(2):
        for i in range(8):
            pltpu.make_async_copy(
                tgb.at[slot, :, pl.ds(i * half, half)],
                tg_h.at[:, pl.ds(i * half, half)],
                ts.at[slot, i],
            ).wait()


COPY_PARTS = 8


def copy_out(*refs):
    sources, targets, sems = refs[:4], refs[4:8], refs[8]
    rows = sources[1].shape[0] // COPY_PARTS
    jobs = [(1, pl.ds(i * rows, rows)) for i in range(COPY_PARTS)]
    jobs = jobs + [(i, pl.ds(0, sources[i].shape[0])) for i in (0, 2, 3)]
    copies = [
        pltpu.make_async_copy(sources[i].at[part], targets[i].at[part], sems.at[n])
        for n, (i, part) in enumerate(jobs)
    ]
    for copy in copies:
        copy.start()
    for copy in copies:
        copy.wait()


def on_device(
    tokens,
    output_gradient,
    frozen_value_weight,
    adapter_down_maps,
    adapter_up_maps,
    block_tenant_ids,
    block_live_rows,
    tenant_owner_slot,
):
    rows, model = tokens.shape
    value = output_gradient.shape[1]
    rank = adapter_down_maps.shape[1]
    nblk = block_tenant_ids.shape[0]
    picks = nblk * rank
    width = model + value
    half = frozen_value_weight.shape[0] // 2
    hbm = pl.BlockSpec(memory_space=pl.ANY)
    smem = pl.BlockSpec(memory_space=pltpu.SMEM)
    vmem = pl.BlockSpec(memory_space=pltpu.VMEM)
    flops = 4 * rows * model * value
    shapes = (
        jax.ShapeDtypeStruct((rows, value), BF16),
        jax.ShapeDtypeStruct((rows, model), BF16),
        jax.ShapeDtypeStruct((1, rank, model), BF16),
        jax.ShapeDtypeStruct((1, rank, value), BF16),
    )
    results = pl.pallas_call(
        kernel,
        out_shape=tuple(pltpu.VMEM(r.shape, r.dtype) for r in shapes),
        in_specs=[hbm] * 5 + [smem, smem, vmem],
        out_specs=(vmem,) * 4,
        scratch_shapes=[
            pltpu.VMEM((rows, model), BF16),
            pltpu.VMEM((rows, value), BF16),
            pltpu.VMEM((2, 4, 8, half, value), BF16),
            pltpu.VMEM((2, 4, rank, width), BF16),
            pltpu.VMEM((4, picks, width), BF16),
            pltpu.VMEM((2, picks, width // 2), BF16),
            pltpu.VMEM((2, picks, width), BF16),
            pltpu.VMEM((picks, width), BF16),
            pltpu.VMEM((4, picks, width), BF16),
            pltpu.VMEM((2, 4, rank, width), BF16),
            pltpu.VMEM((2, rank, width), BF16),
            pltpu.VMEM((2, 2, rank, width), BF16),
            pltpu.VMEM((rank, width), BF16),
            pltpu.VMEM((rank, width), BF16),
            pltpu.VMEM((rank, width), BF16),
            pltpu.VMEM((rows, value), F32),
            pltpu.VMEM((rows, 8 * half), BF16),
            pltpu.VMEM((picks, 8 * half), BF16),
            pltpu.VMEM((2, rows, 8 * half), BF16),
            pltpu.VMEM((rows, value), BF16),
            pltpu.VMEM((4, 8, 128), F32),
            pltpu.VMEM((4 * picks, 8 * rank), BF16),
            pltpu.VMEM((rows, picks), BF16),
            pltpu.VMEM((rows, picks), BF16),
            pltpu.SemaphoreType.DMA((8,)),
            pltpu.SemaphoreType.DMA((2, 8)),
            pltpu.SemaphoreType.DMA((NSEM,)),
            pltpu.SemaphoreType.DMA((NSEM,)),
        ],
        compiler_params=pltpu.CompilerParams(
            collective_id=0, has_side_effects=True, vmem_limit_bytes=56 * 2**20
        ),
        cost_estimate=pl.CostEstimate(
            flops=flops, bytes_accessed=4 * rows * model, transcendentals=0
        ),
    )(
        tokens,
        output_gradient,
        frozen_value_weight,
        adapter_down_maps,
        adapter_up_maps,
        block_tenant_ids,
        block_live_rows,
        tenant_owner_slot.reshape(1, -1),
    )
    return pl.pallas_call(
        copy_out,
        out_shape=shapes,
        in_specs=[hbm] * 4,
        compiler_params=pltpu.CompilerParams(vmem_limit_bytes=4 * 2**20),
        out_specs=(hbm,) * 4,
        scratch_shapes=[pltpu.SemaphoreType.DMA((COPY_PARTS + 3,))],
    )(*results)


def solution(mesh):
    placed = (
        P(("fsdp", "dp"), None),
        P(("fsdp", "dp"), None),
        P("fsdp", None),
        P(("fsdp", "dp"), None, None),
        P(("fsdp", "dp"), None, None),
        P(("fsdp", "dp")),
        P(("fsdp", "dp")),
        P(),
    )
    return jax.shard_map(
        on_device,
        mesh=mesh,
        in_specs=placed,
        out_specs=(
            P(("fsdp", "dp"), None),
            P(("fsdp", "dp"), None),
            P(("fsdp", "dp"), None, None),
            P(("fsdp", "dp"), None, None),
        ),
        check_vma=False,
    )
```

```python
import jax
import jax.numpy as jnp
from jax import lax
from jax.experimental import pallas as pl
from jax.experimental.pallas import tpu as pltpu
from jax.sharding import PartitionSpec as P

ADAPTER_SCALE = 2.0
MESH = pl.DeviceIdType.MESH
F32 = jnp.float32
BF16 = jnp.bfloat16
STEP = 1024
NSEM = 128
NTILE = 256
PARTS = 2
ORDER = (
    "U S D0 D1", "W W M S", "U D0 W W", "D1 U LG D0", "G0 G1 W W", "W W D1 D0",
    "C F G0 F", "G1 W W D1", "D0 G0 W G1", "C F D1 F", "D0 F G0 G1", "F C F D1",
    "L G0 GU G1", "R R G0 GU", "R G1 R R", "GU R R F", "R",
)


def mult(index, of):
    return pl.multiple_of(index, of)


def kernel(
    tok_h, cot_h, w_h, down_h, up_h, ids_s, live_s, owner_v,
    out_h, tg_h, gd_h, gu_h,
    tok, cot, wbuf, src, sel, r1, r2, fin, part, tab, t1, t2, t3, zs, ru, tu,
    acc, xb, meta, smat, lg, low, ls, ss, rs,
):
    rows, model = tok_h.shape
    value = cot_h.shape[1]
    rank = down_h.shape[1]
    nblk = ids_s.shape[0]
    block = rows // nblk
    width = model + value
    picks = nblk * rank
    half = w_h.shape[0] // 2

    f_me = lax.axis_index("fsdp")
    d_me = lax.axis_index("dp")
    zl = f_me // 16
    x = f_me // 4 % 4
    y = f_me % 4
    zh = d_me // 2
    c = d_me % 2
    p = y * (1 - c) + x * c
    q = x * (1 - c) + y * c
    sp = 1 + 3 * c
    sq = 4 - 3 * c
    p_r, p_l, p_o = (p + 1) % 4, (p + 3) % 4, (p + 2) % 4

    def device(zl_, p_, q_):
        return (zl_ * 16 + p_ * sp + q_ * sq, d_me)

    to_z = device(1 - zl, p, q)
    z = zh * 2 + zl

    def along_z(z_):
        return (z_ % 2 * 16 + f_me % 16, z_ // 2 * 2 + c)

    to_zu, to_zd = along_z((z + 1) % 4), along_z((z + 3) % 4)
    to_pr, to_pl = device(zl, p_r, q), device(zl, p_l, q)
    to_qr, to_ql = device(zl, p, (q + 1) % 4), device(zl, p, (q + 3) % 4)
    to_qo = device(zl, p, (q + 2) % 4)
    to_c = (f_me, zh * 2 + 1 - c)

    count = [0]

    def remote(source, target, where):
        i = count[0]
        count[0] += 1
        return pltpu.make_async_remote_copy(
            src_ref=source, dst_ref=target, send_sem=ss.at[i], recv_sem=rs.at[i],
            device_id=where, device_id_type=MESH,
        )

    def start(copies):
        for copy in copies:
            copy.start()

    def recv(copies):
        for copy in copies:
            copy.wait_recv()

    lc_up = pltpu.make_async_copy(up_h.at[0], src.at[zl, p, :, pl.ds(0, value)], ls.at[0])
    lc_down = pltpu.make_async_copy(down_h.at[0], src.at[zl, p, :, pl.ds(value, model)], ls.at[1])
    lc_cot = pltpu.make_async_copy(cot_h, cot, ls.at[2])
    lc_tok = pltpu.make_async_copy(tok_h, tok, ls.at[3])
    w_own = w_h.at[pl.ds(mult(c * half, half), half)]
    lc_w = pltpu.make_async_copy(w_own, wbuf.at[0, 0, zl * 4 + p], ls.at[4])
    start([lc_up, lc_cot, lc_down, lc_w, lc_tok])

    lane = lax.broadcasted_iota(jnp.int32, (8, 128), 1)
    subl = lax.broadcasted_iota(jnp.int32, (8, 128), 0)
    owners = owner_v[...].astype(F32)
    lane1 = lax.broadcasted_iota(jnp.int32, (1, 128), 1)
    mrow = jnp.zeros((8, 128), F32)
    for b in range(nblk):
        slot = jnp.sum(jnp.where(lane1 == ids_s[b], owners, 0.0), axis=1, keepdims=True)
        mrow = jnp.where(subl == b, slot, mrow)
    meta[0] = mrow

    barrier = pltpu.get_barrier_semaphore()
    near = [(a, b) for a in range(2) for b in range(4) if (a, b) != (0, 0)]
    to_near = [device((zl + a) % 2, (p + b) % 4, q) for a, b in near]
    to_q = [to_qr, to_qo, to_ql]
    to_other_z = along_z((z + 3 + 2 * zl) % 4)
    partners = to_near + to_q + [to_other_z, to_c]
    for where in partners:
        pl.semaphore_signal(barrier, inc=1, device_id=where, device_id_type=MESH)
    pl.semaphore_wait(barrier, len(partners))

    def gather(own, at):
        z = [remote(own, at(zl, p), to_z)]
        p1o = [remote(own, at(zl, p), to_pr), remote(own, at(zl, p), to_pl)]
        theirs = at(1 - zl, p)
        p1z = [remote(theirs, theirs, to_pr), remote(theirs, theirs, to_pl)]
        p2 = [
            remote(at(0, p_l), at(0, p_l), to_pr),
            remote(at(1, p_r), at(1, p_r), to_pl),
        ]
        return z, p1o, p1z, p2

    def adapter_at(first, size):
        return lambda zl_, p_: src.at[zl_, p_, :, pl.ds(first, size)]

    m_q = [
        remote(meta.at[0], meta.at[3], to_qr),
        remote(meta.at[0], meta.at[1], to_ql),
        remote(meta.at[0], meta.at[2], to_qo),
    ]

    def scatter_q(first, size):
        h = size // 2
        h0 = first // 2
        q1 = [
            remote(sel.at[2, :, pl.ds(first, h)], r1.at[0, :, pl.ds(h0, h)], to_qr),
            remote(sel.at[2, :, pl.ds(first + h, h)], r1.at[1, :, pl.ds(h0, h)], to_ql),
        ]
        whole = pl.ds(first, size)
        q2 = [
            remote(sel.at[1, :, whole], r2.at[0, :, whole], to_qr),
            remote(sel.at[3, :, whole], r2.at[1, :, whole], to_ql),
        ]
        return q1, q2

    def grads(first, size):
        h = size // 2
        whole = pl.ds(first, size)
        q1 = [
            remote(part.at[0, :, whole], part.at[3, :, whole], to_qr),
            remote(part.at[0, :, whole], part.at[1, :, whole], to_ql),
        ]
        lo, hi = pl.ds(first, h), pl.ds(first + h, h)
        q2 = [
            remote(part.at[3, :, lo], part.at[2, :, lo], to_qr),
            remote(part.at[1, :, hi], part.at[2, :, hi], to_ql),
        ]
        p1 = [
            remote(tab.at[0, p_o, :, whole], t1.at[0, :, whole], to_pr),
            remote(tab.at[1, p_o, :, whole], t1.at[1, :, whole], to_pl),
        ]
        p2 = [
            remote(tab.at[:, p_r, :, whole], t2.at[0, :, :, whole], to_pr),
            remote(tab.at[:, p_l, :, whole], t2.at[1, :, :, whole], to_pl),
        ]
        z = [remote(zs.at[:, whole], t3.at[:, whole], to_z)]
        return q1, q2, p1, p2, z

    def piece(dq, zl_, p_):
        return wbuf.at[0, dq, zl_ * 4 + p_]

    def rows_of(ref, first, size):
        return ref.at[pl.ds(first, size)]

    order = (p, p_l, p_r, p_o)
    held = [w_own] + [piece(0, zl, k) for k in order[1:]]
    w_p1 = [remote(w_own, piece(0, zl, p), to_pr), remote(w_own, piece(0, zl, p), to_pl)]
    w_p2 = [
        remote(rows_of(held[1], 0, half // 2), rows_of(held[1], 0, half // 2), to_pr),
        remote(rows_of(held[2], half // 2, half // 2), rows_of(held[2], half // 2, half // 2), to_pl),
    ]
    w_q1, w_q2, w_z0, w_z1, w_z2 = [], [], [], [], []
    for j in range(4):
        k = order[j]
        up, down = (to_zu, to_zd) if j % 2 == 0 else (to_zd, to_zu)
        w_q1.append([
            remote(held[j], piece(3, zl, k), to_qr),
            remote(held[j], piece(1, zl, k), to_ql),
        ])
        w_z0.append(remote(held[j], piece(0, zl, k), up))
        w_z1.append([
            remote(piece(3, zl, k), piece(3, zl, k), up),
            remote(piece(1, zl, k), piece(1, zl, k), down),
        ])
        if j < 2:
            w_q2.append(remote(piece(3, zl, k), piece(2, zl, k), to_qr))
        else:
            w_q2.append(remote(piece(1, zl, k), piece(2, zl, k), to_ql))
        w_z2.append(remote(piece(2, zl, k), piece(2, zl, k), up))
    w_c = [remote(wbuf.at[0, dq], wbuf.at[1, dq], to_c) for dq in range(4)]

    sent = []

    def go(copies):
        sent.extend(copies)
        start(copies)

    def columns(first, j, step=STEP):
        return pl.ds(mult(first + j * step, 128), step)

    def loop(size, body, step=STEP):
        if size <= step:
            body(0, size)
        else:
            def run(j, carry):
                body(j, step)
                return carry
            lax.fori_loop(0, size // step, run, 0)

    def build_selection():
        lanes = lax.broadcasted_iota(jnp.int32, (1, 128), 1)
        j = lanes // 16
        target = (((j // 4) * 16 + (j % 4) * sp + q * sq) * 4 + d_me).astype(F32)
        same = lax.broadcasted_iota(jnp.int32, (16, 128), 0) == (
            lax.broadcasted_iota(jnp.int32, (16, 128), 1) % 16
        )
        for dq in range(4):
            for b in range(nblk):
                hit = jnp.logical_and(same, meta[dq, b : b + 1, :] == target)
                r0 = (dq * nblk + b) * rank
                smat[r0 : r0 + rank, :] = jnp.where(hit, 1.0, 0.0).astype(BF16)

    def select(first, size):
        def one(j, step):
            cols = columns(first, j, step)
            held = src[:, :, :, cols].reshape(8 * rank, step)
            picked = jnp.dot(smat[...], held, preferred_element_type=F32)
            sel[:, :, cols] = picked.astype(BF16).reshape(4, picks, step)
        loop(size, one)

    def add_halves(first, size):
        h = size // 2
        h0 = first // 2

        def one(j, step):
            from_l, from_r = columns(first, j, step), columns(first + h, j, step)
            got = columns(h0, j, step)
            sel[1, :, from_l] = sel[1, :, from_l] + r1[0, :, got]
            sel[3, :, from_r] = sel[3, :, from_r] + r1[1, :, got]
        loop(h, one)

    def finish_selection(first, size):
        def one(j, step):
            cols = columns(first, j, step)
            fin[:, cols] = sel[0, :, cols] + r2[0, :, cols] + r2[1, :, cols]
        loop(size, one)

    def build_table(first, size):
        def one(j, step):
            cols = columns(first, j, step)
            held = part[:, :, cols].reshape(4 * picks, step)
            total = lax.dot_general(
                smat[...], held, (((0,), (0,)), ((), ())), preferred_element_type=F32
            )
            tab[:, :, :, cols] = total.astype(BF16).reshape(2, 4, rank, step)
        loop(size, one)

    def add_table(first, size):
        def one(j, step):
            cols = columns(first, j, step)
            a = tab[0, p_r, :, cols].astype(F32) + t1[0, :, cols].astype(F32)
            tab[0, p_r, :, cols] = a.astype(BF16)
            a = tab[1, p_l, :, cols].astype(F32) + t1[1, :, cols].astype(F32)
            tab[1, p_l, :, cols] = a.astype(BF16)
        loop(size, one)

    def sum_three(zl_, cols):
        return (
            tab[zl_, p, :, cols].astype(F32)
            + t2[0, zl_, :, cols].astype(F32)
            + t2[1, zl_, :, cols].astype(F32)
        )

    def send_table(first, size):
        def one(j, step):
            cols = columns(first, j, step)
            zs[:, cols] = sum_three(1 - zl, cols).astype(BF16)
        loop(size, one)

    def finish_table(first, size):
        def one(j, step):
            cols = columns(first, j, step)
            total = sum_three(zl, cols) + t3[:, cols].astype(F32)
            gd_h[0, :, columns(first - value, j, step)] = total.astype(BF16)
        loop(size, one)

    def live_mask(shape):
        r = lax.broadcasted_iota(jnp.int32, shape, 0)
        limit = jnp.zeros(shape, jnp.int32)
        for b in range(nblk):
            limit = jnp.where(r // block == b, live_s[b] + b * block, limit)
        return r < limit

    def block_mask():
        r = lax.broadcasted_iota(jnp.int32, (rows, picks), 0)
        k = lax.broadcasted_iota(jnp.int32, (rows, picks), 1)
        return jnp.logical_and(r // block == k // rank, live_mask((rows, picks)))

    def place(g, dq, i):
        spg = sp + g * (sq - sp)
        sqg = sq + g * (sp - sq)
        qg = q + g * (p - q)
        hg = c + g * (1 - 2 * c)
        f = (i // 4) * 16 + (i % 4) * spg + ((qg + dq) % 4) * sqg
        return mult(f * (2 * half) + hg * half, half)

    def forward(g, dq, first):
        for i in range(8):
            xb[:, i * half : (i + 1) * half] = tok[:, pl.ds(place(g, dq, i), half)]
        for n in range(value // NTILE):
            cols = pl.ds(n * NTILE, NTILE)
            w = wbuf[g, dq, :, :, cols].reshape(8 * half, NTILE)
            got = jnp.dot(xb[...], w, preferred_element_type=F32)
            acc[:, cols] = got if first else acc[:, cols] + got

    def backward(g, dq):
        for m in range(4):
            w = wbuf[g, dq, 2 * m : 2 * m + 2, :, :].reshape(2 * half, value)
            here = [place(g, dq, 2 * m + i) for i in range(2)]
            maps = [fin[:, pl.ds(mult(value + at, half), half)] for at in here]
            got = lax.dot_general(
                cot[...], w, (((1,), (1,)), ((), ())), preferred_element_type=F32
            )
            got = got + jnp.dot(
                lg[...], jnp.concatenate(maps, axis=1), preferred_element_type=F32
            )
            got = got.astype(BF16)
            for i in range(2):
                tg_h[:, pl.ds(here[i], half)] = got[:, i * half : (i + 1) * half]

    def adapter_chain(own, first, size):
        z1, p1o, p1z, p2 = gather(own, adapter_at(first, size))
        q1, q2 = scatter_q(first, size)
        go(z1 + p1o)
        yield
        recv(z1)
        go(p1z)
        yield
        recv(p1o + p1z)
        go(p2)
        yield
        recv(p2)
        select(first, size)
        go(q1)
        yield
        recv(q1)
        add_halves(first, size)
        go(q2)
        yield
        recv(q2)
        finish_selection(first, size)
        yield

    def up_chain():
        at = pl.ds(0, value)
        spread = [
            remote(up_h.at[0], src.at[zl, p, :, at], where) for where in to_near
        ]
        go(spread)
        yield
        recv(spread)
        select(0, value)
        deliver = [
            remote(sel.at[i + 1, :, at], ru.at[i], to_q[i]) for i in range(3)
        ]
        go(deliver)
        yield
        recv(deliver)
        fin[:, at] = sel[0, :, at] + ru[0] + ru[1] + ru[2]
        yield

    def up_gradient_chain():
        at = pl.ds(0, value)
        got = lax.dot_general(
            low[...], cot[...], (((0,), (0,)), ((), ())), preferred_element_type=F32
        )
        part[0, :, at] = (ADAPTER_SCALE * got).astype(BF16)
        spread = [
            remote(part.at[0, :, at], part.at[3 - i, :, at], to_q[i]) for i in range(3)
        ]
        go(spread)
        yield
        recv(spread)
        build_table(0, value)
        collect = [
            remote(tab.at[(zl + a) % 2, (p + b) % 4, :, at], tu.at[i], to_near[i])
            for i, (a, b) in enumerate(near)
        ]
        go(collect)
        yield
        recv(collect)
        total = tab[zl, p, :, at].astype(F32)
        for i in range(7):
            total = total + tu[i].astype(F32)
        gu_h[0] = total.astype(BF16)
        yield

    def gradient_chain(first, size, make):
        q1, q2, p1, p2, z1 = grads(first, size)
        make()
        go(q1)
        yield
        recv(q1)
        go(q2)
        yield
        recv(q2)
        build_table(first, size)
        go(p1)
        yield
        recv(p1)
        add_table(first, size)
        go(p2)
        yield
        recv(p2)
        send_table(first, size)
        go(z1)
        yield
        recv(z1)
        finish_table(first, size)
        yield

    def weight_chain():
        go(w_p1)
        yield
        go(w_q1[0] + [w_z0[0]])
        yield
        recv([w_p1[0]])
        go([w_p2[0]] + w_q1[1] + [w_z0[1]])
        yield
        recv([w_p1[1]])
        go([w_p2[1]] + w_q1[2] + [w_z0[2]])
        yield
        recv(w_p2)
        go(w_q1[3] + [w_z0[3]])
        yield
        for j in range(4):
            recv(w_q1[j])
            go(w_z1[j] + [w_q2[j]])
            yield
        for j in (0, 2):
            recv(w_q2[j : j + 2])
            go(w_z2[j : j + 2])
            yield

    def core_chain():
        lc_w.wait()
        recv(w_z0)
        go([w_c[0]])
        yield
        for pair in w_z1:
            recv(pair)
        go([w_c[1], w_c[3]])
        yield
        recv(w_z2)
        go([w_c[2]])
        yield

    batches = ((0, 0), (1, 0), (0, 1), (0, 3), (1, 1), (1, 3), (0, 2), (1, 2))

    def forward_chain():
        for n, (g, dq) in enumerate(batches):
            if g == 1:
                recv([w_c[dq]])
            forward(g, dq, n == 0)
            yield

    def backward_chain():
        for g, dq in batches:
            backward(g, dq)
            yield

    def mask_chain():
        lc_cot.wait()
        lc_tok.wait()
        cot[...] = jnp.where(live_mask((rows, value)), cot[...].astype(F32), 0.0).astype(BF16)
        lc_up.wait()
        lc_down.wait()
        yield

    def meta_chain():
        go(m_q)
        yield
        recv(m_q)
        build_selection()
        yield

    def low_gradient_chain():
        back = lax.dot_general(
            cot[...], fin[:, pl.ds(0, value)], (((1,), (1,)), ((), ())), preferred_element_type=F32
        )
        lg[...] = jnp.where(block_mask(), ADAPTER_SCALE * back, 0.0).astype(BF16)
        yield

    def down_parts(first, size):
        def make():
            def down_part(j, step):
                got = lax.dot_general(
                    lg[...], tok[:, columns(first - value, j, step)], (((0,), (0,)), ((), ())),
                    preferred_element_type=F32,
                )
                part[0, :, columns(first, j, step)] = got.astype(BF16)
            loop(size, down_part)
        return make

    def low_chain():
        def low_part(j, total):
            return total + lax.dot_general(
                tok[:, columns(0, j)], fin[:, columns(value, j)], (((1,), (1,)), ((), ())),
                preferred_element_type=F32,
            )
        total = lax.fori_loop(0, model // STEP, low_part, jnp.zeros((rows, picks), F32))
        low[...] = jnp.where(block_mask(), total, 0.0).astype(BF16)
        yield

    chains = {
        "U": up_chain(),
        "GU": up_gradient_chain(),
        "W": weight_chain(),
        "C": core_chain(),
        "F": forward_chain(),
        "R": backward_chain(),
        "M": mask_chain(),
        "S": meta_chain(),
        "LG": low_gradient_chain(),
        "L": low_chain(),
    }
    size = model // PARTS
    for k in range(PARTS):
        own = down_h.at[0, :, pl.ds(k * size, size)]
        chains["D%d" % k] = adapter_chain(own, value + k * size, size)
        chains["G%d" % k] = gradient_chain(
            value + k * size, size, down_parts(value + k * size, size)
        )
    for name in " ".join(ORDER).split():
        next(chains[name])

    for n in range(value // NTILE):
        cols = pl.ds(n * NTILE, NTILE)
        total = acc[:, cols] + ADAPTER_SCALE * jnp.dot(
            low[...], fin[:, cols], preferred_element_type=F32
        )
        out_h[:, cols] = jnp.where(live_mask((rows, NTILE)), total, 0.0).astype(BF16)

    for copy in sent:
        copy.wait_send()


COPY_PARTS = 8


def copy_out(*refs):
    sources, targets, sems = refs[:4], refs[4:8], refs[8]
    rows = sources[1].shape[0] // COPY_PARTS
    jobs = [(1, pl.ds(i * rows, rows)) for i in range(COPY_PARTS)]
    jobs = jobs + [(i, pl.ds(0, sources[i].shape[0])) for i in (0, 2, 3)]
    copies = [
        pltpu.make_async_copy(sources[i].at[part], targets[i].at[part], sems.at[n])
        for n, (i, part) in enumerate(jobs)
    ]
    for copy in copies:
        copy.start()
    for copy in copies:
        copy.wait()


def on_device(
    tokens,
    output_gradient,
    frozen_value_weight,
    adapter_down_maps,
    adapter_up_maps,
    block_tenant_ids,
    block_live_rows,
    tenant_owner_slot,
):
    rows, model = tokens.shape
    value = output_gradient.shape[1]
    rank = adapter_down_maps.shape[1]
    nblk = block_tenant_ids.shape[0]
    picks = nblk * rank
    width = model + value
    half = frozen_value_weight.shape[0] // 2
    hbm = pl.BlockSpec(memory_space=pl.ANY)
    smem = pl.BlockSpec(memory_space=pltpu.SMEM)
    vmem = pl.BlockSpec(memory_space=pltpu.VMEM)
    flops = 4 * rows * model * value
    shapes = (
        jax.ShapeDtypeStruct((rows, value), BF16),
        jax.ShapeDtypeStruct((rows, model), BF16),
        jax.ShapeDtypeStruct((1, rank, model), BF16),
        jax.ShapeDtypeStruct((1, rank, value), BF16),
    )
    results = pl.pallas_call(
        kernel,
        out_shape=tuple(pltpu.VMEM(r.shape, r.dtype) for r in shapes),
        in_specs=[hbm] * 5 + [smem, smem, vmem],
        out_specs=(vmem,) * 4,
        scratch_shapes=[
            pltpu.VMEM((rows, model), BF16),
            pltpu.VMEM((rows, value), BF16),
            pltpu.VMEM((2, 4, 8, half, value), BF16),
            pltpu.VMEM((2, 4, rank, width), BF16),
            pltpu.VMEM((4, picks, width), BF16),
            pltpu.VMEM((2, picks, width // 2), BF16),
            pltpu.VMEM((2, picks, width), BF16),
            pltpu.VMEM((picks, width), BF16),
            pltpu.VMEM((4, picks, width), BF16),
            pltpu.VMEM((2, 4, rank, width), BF16),
            pltpu.VMEM((2, rank, width), BF16),
            pltpu.VMEM((2, 2, rank, width), BF16),
            pltpu.VMEM((rank, width), BF16),
            pltpu.VMEM((rank, width), BF16),
            pltpu.VMEM((3, picks, value), BF16),
            pltpu.VMEM((7, rank, value), BF16),
            pltpu.VMEM((rows, value), F32),
            pltpu.VMEM((rows, 8 * half), BF16),
            pltpu.VMEM((4, 8, 128), F32),
            pltpu.VMEM((4 * picks, 8 * rank), BF16),
            pltpu.VMEM((rows, picks), BF16),
            pltpu.VMEM((rows, picks), BF16),
            pltpu.SemaphoreType.DMA((8,)),
            pltpu.SemaphoreType.DMA((NSEM,)),
            pltpu.SemaphoreType.DMA((NSEM,)),
        ],
        compiler_params=pltpu.CompilerParams(
            collective_id=0, has_side_effects=True, vmem_limit_bytes=56 * 2**20
        ),
        cost_estimate=pl.CostEstimate(
            flops=flops, bytes_accessed=4 * rows * model, transcendentals=0
        ),
    )(
        tokens,
        output_gradient,
        frozen_value_weight,
        adapter_down_maps,
        adapter_up_maps,
        block_tenant_ids,
        block_live_rows,
        tenant_owner_slot.reshape(1, -1),
    )
    return pl.pallas_call(
        copy_out,
        out_shape=shapes,
        in_specs=[hbm] * 4,
        compiler_params=pltpu.CompilerParams(vmem_limit_bytes=4 * 2**20),
        out_specs=(hbm,) * 4,
        scratch_shapes=[pltpu.SemaphoreType.DMA((COPY_PARTS + 3,))],
    )(*results)


def solution(mesh):
    placed = (
        P(("fsdp", "dp"), None),
        P(("fsdp", "dp"), None),
        P("fsdp", None),
        P(("fsdp", "dp"), None, None),
        P(("fsdp", "dp"), None, None),
        P(("fsdp", "dp")),
        P(("fsdp", "dp")),
        P(),
    )
    return jax.shard_map(
        on_device,
        mesh=mesh,
        in_specs=placed,
        out_specs=(
            P(("fsdp", "dp"), None),
            P(("fsdp", "dp"), None),
            P(("fsdp", "dp"), None, None),
            P(("fsdp", "dp"), None, None),
        ),
        check_vma=False,
    )
```

```python
import jax
import jax.numpy as jnp
from jax import lax
from jax.experimental import pallas as pl
from jax.experimental.pallas import tpu as pltpu
from jax.sharding import PartitionSpec as P

ADAPTER_SCALE = 2.0
MESH = pl.DeviceIdType.MESH
F32 = jnp.float32
BF16 = jnp.bfloat16
STEP = 1024
NSEM = 128
NTILE = 512
PARTS = 2
ORDER = (
    "U S W D0", "W M S U", "W D1 W D1", "U D0 W LG", "G1 W G0 D1", "C D0 W F",
    "F W W G1", "G0 D0 D1 W", "G1 G0 C D0", "W F F D1", "F F D0 G1", "G0 C F D1",
    "L GU G1 F", "R R G0 R", "R G1 GU R", "R R R GU", "G0",
)


def mult(index, of):
    return pl.multiple_of(index, of)


def kernel(
    tok_h, cot_h, w_h, down_h, up_h, ids_s, live_s, owner_v,
    out_h, tg_h, gd_h, gu_h,
    tok, cot, wbuf, src, sel, r1, r2, fin, part, tab, t1, t2, t3, zs, ru, tu,
    acc, xb, meta, smat, lg, low, ls, ss, rs,
):
    rows, model = tok_h.shape
    value = cot_h.shape[1]
    rank = down_h.shape[1]
    nblk = ids_s.shape[0]
    block = rows // nblk
    width = model + value
    picks = nblk * rank
    half = w_h.shape[0] // 2

    f_me = lax.axis_index("fsdp")
    d_me = lax.axis_index("dp")
    zl = f_me // 16
    x = f_me // 4 % 4
    y = f_me % 4
    zh = d_me // 2
    c = d_me % 2
    p = y * (1 - c) + x * c
    q = x * (1 - c) + y * c
    sp = 1 + 3 * c
    sq = 4 - 3 * c
    p_r, p_l, p_o = (p + 1) % 4, (p + 3) % 4, (p + 2) % 4

    def device(zl_, p_, q_):
        return (zl_ * 16 + p_ * sp + q_ * sq, d_me)

    to_z = device(1 - zl, p, q)
    z = zh * 2 + zl

    def along_z(z_):
        return (z_ % 2 * 16 + f_me % 16, z_ // 2 * 2 + c)

    to_zu, to_zd = along_z((z + 1) % 4), along_z((z + 3) % 4)
    to_pr, to_pl = device(zl, p_r, q), device(zl, p_l, q)
    to_qr, to_ql = device(zl, p, (q + 1) % 4), device(zl, p, (q + 3) % 4)
    to_qo = device(zl, p, (q + 2) % 4)
    to_c = (f_me, zh * 2 + 1 - c)

    count = [0]

    def remote(source, target, where):
        i = count[0]
        count[0] += 1
        return pltpu.make_async_remote_copy(
            src_ref=source, dst_ref=target, send_sem=ss.at[i], recv_sem=rs.at[i],
            device_id=where, device_id_type=MESH,
        )

    def start(copies):
        for copy in copies:
            copy.start()

    def recv(copies):
        for copy in copies:
            copy.wait_recv()

    lc_up = pltpu.make_async_copy(up_h.at[0], src.at[zl, p, :, pl.ds(0, value)], ls.at[0])
    lc_down = pltpu.make_async_copy(down_h.at[0], src.at[zl, p, :, pl.ds(value, model)], ls.at[1])
    lc_cot = pltpu.make_async_copy(cot_h, cot, ls.at[2])
    lc_tok = pltpu.make_async_copy(tok_h, tok, ls.at[3])
    w_own = w_h.at[pl.ds(mult(c * half, half), half)]
    lc_w = pltpu.make_async_copy(w_own, wbuf.at[0, 0, zl * 4 + p], ls.at[4])
    start([lc_up, lc_cot, lc_down, lc_w, lc_tok])

    lane = lax.broadcasted_iota(jnp.int32, (8, 128), 1)
    subl = lax.broadcasted_iota(jnp.int32, (8, 128), 0)
    owners = owner_v[...].astype(F32)
    lane1 = lax.broadcasted_iota(jnp.int32, (1, 128), 1)
    mrow = jnp.zeros((8, 128), F32)
    for b in range(nblk):
        slot = jnp.sum(jnp.where(lane1 == ids_s[b], owners, 0.0), axis=1, keepdims=True)
        mrow = jnp.where(subl == b, slot, mrow)
    meta[0] = mrow

    barrier = pltpu.get_barrier_semaphore()
    near = [(a, b) for a in range(2) for b in range(4) if (a, b) != (0, 0)]
    to_near = [device((zl + a) % 2, (p + b) % 4, q) for a, b in near]
    to_q = [to_qr, to_qo, to_ql]
    to_other_z = along_z((z + 3 + 2 * zl) % 4)
    partners = to_near + to_q + [to_other_z, to_c]
    for where in partners:
        pl.semaphore_signal(barrier, inc=1, device_id=where, device_id_type=MESH)
    pl.semaphore_wait(barrier, len(partners))

    def gather(own, at):
        z = [remote(own, at(zl, p), to_z)]
        p1o = [remote(own, at(zl, p), to_pr), remote(own, at(zl, p), to_pl)]
        theirs = at(1 - zl, p)
        p1z = [remote(theirs, theirs, to_pr), remote(theirs, theirs, to_pl)]
        p2 = [
            remote(at(0, p_l), at(0, p_l), to_pr),
            remote(at(1, p_r), at(1, p_r), to_pl),
        ]
        return z, p1o, p1z, p2

    def adapter_at(first, size):
        return lambda zl_, p_: src.at[zl_, p_, :, pl.ds(first, size)]

    m_q = [
        remote(meta.at[0], meta.at[3], to_qr),
        remote(meta.at[0], meta.at[1], to_ql),
        remote(meta.at[0], meta.at[2], to_qo),
    ]

    def scatter_q(first, size):
        h = size // 2
        h0 = first // 2
        q1 = [
            remote(sel.at[2, :, pl.ds(first, h)], r1.at[0, :, pl.ds(h0, h)], to_qr),
            remote(sel.at[2, :, pl.ds(first + h, h)], r1.at[1, :, pl.ds(h0, h)], to_ql),
        ]
        whole = pl.ds(first, size)
        q2 = [
            remote(sel.at[1, :, whole], r2.at[0, :, whole], to_qr),
            remote(sel.at[3, :, whole], r2.at[1, :, whole], to_ql),
        ]
        return q1, q2

    def grads(first, size):
        h = size // 2
        whole = pl.ds(first, size)
        q1 = [
            remote(part.at[0, :, whole], part.at[3, :, whole], to_qr),
            remote(part.at[0, :, whole], part.at[1, :, whole], to_ql),
        ]
        lo, hi = pl.ds(first, h), pl.ds(first + h, h)
        q2 = [
            remote(part.at[3, :, lo], part.at[2, :, lo], to_qr),
            remote(part.at[1, :, hi], part.at[2, :, hi], to_ql),
        ]
        p1 = [
            remote(tab.at[0, p_o, :, whole], t1.at[0, :, whole], to_pr),
            remote(tab.at[1, p_o, :, whole], t1.at[1, :, whole], to_pl),
        ]
        p2 = [
            remote(tab.at[:, p_r, :, whole], t2.at[0, :, :, whole], to_pr),
            remote(tab.at[:, p_l, :, whole], t2.at[1, :, :, whole], to_pl),
        ]
        z = [remote(zs.at[:, whole], t3.at[:, whole], to_z)]
        return q1, q2, p1, p2, z

    def piece(dq, zl_, p_):
        return wbuf.at[0, dq, zl_ * 4 + p_]

    def rows_of(ref, first, size):
        return ref.at[pl.ds(first, size)]

    order = (p, p_l, p_r, p_o)
    held = [w_own] + [piece(0, zl, k) for k in order[1:]]
    w_p1 = [remote(w_own, piece(0, zl, p), to_pr), remote(w_own, piece(0, zl, p), to_pl)]
    w_p2 = [
        remote(rows_of(held[1], 0, half // 2), rows_of(held[1], 0, half // 2), to_pr),
        remote(rows_of(held[2], half // 2, half // 2), rows_of(held[2], half // 2, half // 2), to_pl),
    ]
    w_q1, w_q2, w_z0, w_z1, w_z2 = [], [], [], [], []
    for j in range(4):
        k = order[j]
        up, down = (to_zu, to_zd) if j % 2 == 0 else (to_zd, to_zu)
        w_q1.append([
            remote(held[j], piece(3, zl, k), to_qr),
            remote(held[j], piece(1, zl, k), to_ql),
        ])
        w_z0.append(remote(held[j], piece(0, zl, k), up))
        w_z1.append([
            remote(piece(3, zl, k), piece(3, zl, k), up),
            remote(piece(1, zl, k), piece(1, zl, k), down),
        ])
        if j < 2:
            w_q2.append(remote(piece(3, zl, k), piece(2, zl, k), to_qr))
        else:
            w_q2.append(remote(piece(1, zl, k), piece(2, zl, k), to_ql))
        w_z2.append(remote(piece(2, zl, k), piece(2, zl, k), up))
    w_c = [remote(wbuf.at[0, dq], wbuf.at[1, dq], to_c) for dq in range(4)]

    sent = []

    def go(copies):
        sent.extend(copies)
        start(copies)

    def columns(first, j, step=STEP):
        return pl.ds(mult(first + j * step, 128), step)

    def loop(size, body, step=STEP):
        if size <= step:
            body(0, size)
        else:
            def run(j, carry):
                body(j, step)
                return carry
            lax.fori_loop(0, size // step, run, 0)

    def build_selection():
        lanes = lax.broadcasted_iota(jnp.int32, (1, 128), 1)
        j = lanes // 16
        target = (((j // 4) * 16 + (j % 4) * sp + q * sq) * 4 + d_me).astype(F32)
        same = lax.broadcasted_iota(jnp.int32, (16, 128), 0) == (
            lax.broadcasted_iota(jnp.int32, (16, 128), 1) % 16
        )
        for dq in range(4):
            for b in range(nblk):
                hit = jnp.logical_and(same, meta[dq, b : b + 1, :] == target)
                r0 = (dq * nblk + b) * rank
                smat[r0 : r0 + rank, :] = jnp.where(hit, 1.0, 0.0).astype(BF16)

    def select(first, size):
        def one(j, step):
            cols = columns(first, j, step)
            held = src[:, :, :, cols].reshape(8 * rank, step)
            picked = jnp.dot(smat[...], held, preferred_element_type=F32)
            sel[:, :, cols] = picked.astype(BF16).reshape(4, picks, step)
        loop(size, one)

    def add_halves(first, size):
        h = size // 2
        h0 = first // 2

        def one(j, step):
            from_l, from_r = columns(first, j, step), columns(first + h, j, step)
            got = columns(h0, j, step)
            sel[1, :, from_l] = sel[1, :, from_l] + r1[0, :, got]
            sel[3, :, from_r] = sel[3, :, from_r] + r1[1, :, got]
        loop(h, one)

    def finish_selection(first, size):
        def one(j, step):
            cols = columns(first, j, step)
            fin[:, cols] = sel[0, :, cols] + r2[0, :, cols] + r2[1, :, cols]
        loop(size, one)

    def build_table(first, size):
        def one(j, step):
            cols = columns(first, j, step)
            held = part[:, :, cols].reshape(4 * picks, step)
            total = lax.dot_general(
                smat[...], held, (((0,), (0,)), ((), ())), preferred_element_type=F32
            )
            tab[:, :, :, cols] = total.astype(BF16).reshape(2, 4, rank, step)
        loop(size, one)

    def add_table(first, size):
        def one(j, step):
            cols = columns(first, j, step)
            a = tab[0, p_r, :, cols].astype(F32) + t1[0, :, cols].astype(F32)
            tab[0, p_r, :, cols] = a.astype(BF16)
            a = tab[1, p_l, :, cols].astype(F32) + t1[1, :, cols].astype(F32)
            tab[1, p_l, :, cols] = a.astype(BF16)
        loop(size, one)

    def sum_three(zl_, cols):
        return (
            tab[zl_, p, :, cols].astype(F32)
            + t2[0, zl_, :, cols].astype(F32)
            + t2[1, zl_, :, cols].astype(F32)
        )

    def send_table(first, size):
        def one(j, step):
            cols = columns(first, j, step)
            zs[:, cols] = sum_three(1 - zl, cols).astype(BF16)
        loop(size, one)

    def finish_table(first, size):
        def one(j, step):
            cols = columns(first, j, step)
            total = sum_three(zl, cols) + t3[:, cols].astype(F32)
            gd_h[0, :, columns(first - value, j, step)] = total.astype(BF16)
        loop(size, one)

    def live_mask(shape):
        r = lax.broadcasted_iota(jnp.int32, shape, 0)
        limit = jnp.zeros(shape, jnp.int32)
        for b in range(nblk):
            limit = jnp.where(r // block == b, live_s[b] + b * block, limit)
        return r < limit

    def block_mask():
        r = lax.broadcasted_iota(jnp.int32, (rows, picks), 0)
        k = lax.broadcasted_iota(jnp.int32, (rows, picks), 1)
        return jnp.logical_and(r // block == k // rank, live_mask((rows, picks)))

    def place(g, dq, i):
        spg = sp + g * (sq - sp)
        sqg = sq + g * (sp - sq)
        qg = q + g * (p - q)
        hg = c + g * (1 - 2 * c)
        f = (i // 4) * 16 + (i % 4) * spg + ((qg + dq) % 4) * sqg
        return mult(f * (2 * half) + hg * half, half)

    def forward(g, dq, first):
        for i in range(8):
            xb[:, i * half : (i + 1) * half] = tok[:, pl.ds(place(g, dq, i), half)]
        for n in range(value // NTILE):
            cols = pl.ds(n * NTILE, NTILE)
            w = wbuf[g, dq, :, :, cols].reshape(8 * half, NTILE)
            got = jnp.dot(xb[...], w, preferred_element_type=F32)
            acc[:, cols] = got if first else acc[:, cols] + got

    def backward(g, dq):
        for m in range(4):
            w = wbuf[g, dq, 2 * m : 2 * m + 2, :, :].reshape(2 * half, value)
            here = [place(g, dq, 2 * m + i) for i in range(2)]
            maps = [fin[:, pl.ds(mult(value + at, half), half)] for at in here]
            got = lax.dot_general(
                cot[...], w, (((1,), (1,)), ((), ())), preferred_element_type=F32
            )
            got = got + jnp.dot(
                lg[...], jnp.concatenate(maps, axis=1), preferred_element_type=F32
            )
            got = got.astype(BF16)
            for i in range(2):
                tg_h[:, pl.ds(here[i], half)] = got[:, i * half : (i + 1) * half]

    def adapter_chain(own, first, size):
        z1, p1o, p1z, p2 = gather(own, adapter_at(first, size))
        q1, q2 = scatter_q(first, size)
        go(z1 + p1o)
        yield
        recv(z1)
        go(p1z)
        yield
        recv(p1o + p1z)
        go(p2)
        yield
        recv(p2)
        select(first, size)
        go(q1)
        yield
        recv(q1)
        add_halves(first, size)
        go(q2)
        yield
        recv(q2)
        finish_selection(first, size)
        yield

    def up_chain():
        at = pl.ds(0, value)
        spread = [
            remote(up_h.at[0], src.at[zl, p, :, at], where) for where in to_near
        ]
        go(spread)
        yield
        recv(spread)
        select(0, value)
        deliver = [
            remote(sel.at[i + 1, :, at], ru.at[i], to_q[i]) for i in range(3)
        ]
        go(deliver)
        yield
        recv(deliver)
        fin[:, at] = sel[0, :, at] + ru[0] + ru[1] + ru[2]
        yield

    def up_gradient_chain():
        at = pl.ds(0, value)
        got = lax.dot_general(
            low[...], cot[...], (((0,), (0,)), ((), ())), preferred_element_type=F32
        )
        part[0, :, at] = (ADAPTER_SCALE * got).astype(BF16)
        spread = [
            remote(part.at[0, :, at], part.at[3 - i, :, at], to_q[i]) for i in range(3)
        ]
        go(spread)
        yield
        recv(spread)
        build_table(0, value)
        collect = [
            remote(tab.at[(zl + a) % 2, (p + b) % 4, :, at], tu.at[i], to_near[i])
            for i, (a, b) in enumerate(near)
        ]
        go(collect)
        yield
        recv(collect)
        total = tab[zl, p, :, at].astype(F32)
        for i in range(7):
            total = total + tu[i].astype(F32)
        gu_h[0] = total.astype(BF16)
        yield

    def gradient_chain(first, size, make):
        q1, q2, p1, p2, z1 = grads(first, size)
        make()
        go(q1)
        yield
        recv(q1)
        go(q2)
        yield
        recv(q2)
        build_table(first, size)
        go(p1)
        yield
        recv(p1)
        add_table(first, size)
        go(p2)
        yield
        recv(p2)
        send_table(first, size)
        go(z1)
        yield
        recv(z1)
        finish_table(first, size)
        yield

    def weight_chain():
        go(w_p1)
        yield
        go(w_q1[0] + [w_z0[0]])
        yield
        recv([w_p1[0]])
        go([w_p2[0]] + w_q1[1] + [w_z0[1]])
        yield
        recv([w_p1[1]])
        go([w_p2[1]] + w_q1[2] + [w_z0[2]])
        yield
        recv(w_p2)
        go(w_q1[3] + [w_z0[3]])
        yield
        for j in range(4):
            recv(w_q1[j])
            go(w_z1[j] + [w_q2[j]])
            yield
        for j in (0, 2):
            recv(w_q2[j : j + 2])
            go(w_z2[j : j + 2])
            yield

    def core_chain():
        lc_w.wait()
        recv(w_z0)
        go([w_c[0]])
        yield
        for pair in w_z1:
            recv(pair)
        go([w_c[1], w_c[3]])
        yield
        recv(w_z2)
        go([w_c[2]])
        yield

    batches = ((0, 0), (1, 0), (0, 1), (0, 3), (1, 1), (1, 3), (0, 2), (1, 2))

    def forward_chain():
        for n, (g, dq) in enumerate(batches):
            if g == 1:
                recv([w_c[dq]])
            forward(g, dq, n == 0)
            yield

    def backward_chain():
        for g, dq in batches:
            backward(g, dq)
            yield

    def mask_chain():
        lc_cot.wait()
        lc_tok.wait()
        cot[...] = jnp.where(live_mask((rows, value)), cot[...].astype(F32), 0.0).astype(BF16)
        lc_up.wait()
        lc_down.wait()
        yield

    def meta_chain():
        go(m_q)
        yield
        recv(m_q)
        build_selection()
        yield

    def low_gradient_chain():
        back = lax.dot_general(
            cot[...], fin[:, pl.ds(0, value)], (((1,), (1,)), ((), ())), preferred_element_type=F32
        )
        lg[...] = jnp.where(block_mask(), ADAPTER_SCALE * back, 0.0).astype(BF16)
        yield

    def down_parts(first, size):
        def make():
            def down_part(j, step):
                got = lax.dot_general(
                    lg[...], tok[:, columns(first - value, j, step)], (((0,), (0,)), ((), ())),
                    preferred_element_type=F32,
                )
                part[0, :, columns(first, j, step)] = got.astype(BF16)
            loop(size, down_part)
        return make

    def low_chain():
        def low_part(j, total):
            return total + lax.dot_general(
                tok[:, columns(0, j)], fin[:, columns(value, j)], (((1,), (1,)), ((), ())),
                preferred_element_type=F32,
            )
        total = lax.fori_loop(0, model // STEP, low_part, jnp.zeros((rows, picks), F32))
        low[...] = jnp.where(block_mask(), total, 0.0).astype(BF16)
        yield

    chains = {
        "U": up_chain(),
        "GU": up_gradient_chain(),
        "W": weight_chain(),
        "C": core_chain(),
        "F": forward_chain(),
        "R": backward_chain(),
        "M": mask_chain(),
        "S": meta_chain(),
        "LG": low_gradient_chain(),
        "L": low_chain(),
    }
    size = model // PARTS
    for k in range(PARTS):
        own = down_h.at[0, :, pl.ds(k * size, size)]
        chains["D%d" % k] = adapter_chain(own, value + k * size, size)
        chains["G%d" % k] = gradient_chain(
            value + k * size, size, down_parts(value + k * size, size)
        )
    for name in " ".join(ORDER).split():
        next(chains[name])

    for n in range(value // NTILE):
        cols = pl.ds(n * NTILE, NTILE)
        total = acc[:, cols] + ADAPTER_SCALE * jnp.dot(
            low[...], fin[:, cols], preferred_element_type=F32
        )
        out_h[:, cols] = jnp.where(live_mask((rows, NTILE)), total, 0.0).astype(BF16)

    for copy in sent:
        copy.wait_send()


COPY_PARTS = 8


def copy_out(*refs):
    sources, targets, sems = refs[:4], refs[4:8], refs[8]
    rows = sources[1].shape[0] // COPY_PARTS
    jobs = [(1, pl.ds(i * rows, rows)) for i in range(COPY_PARTS)]
    jobs = jobs + [(i, pl.ds(0, sources[i].shape[0])) for i in (0, 2, 3)]
    copies = [
        pltpu.make_async_copy(sources[i].at[part], targets[i].at[part], sems.at[n])
        for n, (i, part) in enumerate(jobs)
    ]
    for copy in copies:
        copy.start()
    for copy in copies:
        copy.wait()


def on_device(
    tokens,
    output_gradient,
    frozen_value_weight,
    adapter_down_maps,
    adapter_up_maps,
    block_tenant_ids,
    block_live_rows,
    tenant_owner_slot,
):
    rows, model = tokens.shape
    value = output_gradient.shape[1]
    rank = adapter_down_maps.shape[1]
    nblk = block_tenant_ids.shape[0]
    picks = nblk * rank
    width = model + value
    half = frozen_value_weight.shape[0] // 2
    hbm = pl.BlockSpec(memory_space=pl.ANY)
    smem = pl.BlockSpec(memory_space=pltpu.SMEM)
    vmem = pl.BlockSpec(memory_space=pltpu.VMEM)
    flops = 4 * rows * model * value
    shapes = (
        jax.ShapeDtypeStruct((rows, value), BF16),
        jax.ShapeDtypeStruct((rows, model), BF16),
        jax.ShapeDtypeStruct((1, rank, model), BF16),
        jax.ShapeDtypeStruct((1, rank, value), BF16),
    )
    results = pl.pallas_call(
        kernel,
        out_shape=tuple(pltpu.VMEM(r.shape, r.dtype) for r in shapes),
        in_specs=[hbm] * 5 + [smem, smem, vmem],
        out_specs=(vmem,) * 4,
        scratch_shapes=[
            pltpu.VMEM((rows, model), BF16),
            pltpu.VMEM((rows, value), BF16),
            pltpu.VMEM((2, 4, 8, half, value), BF16),
            pltpu.VMEM((2, 4, rank, width), BF16),
            pltpu.VMEM((4, picks, width), BF16),
            pltpu.VMEM((2, picks, width // 2), BF16),
            pltpu.VMEM((2, picks, width), BF16),
            pltpu.VMEM((picks, width), BF16),
            pltpu.VMEM((4, picks, width), BF16),
            pltpu.VMEM((2, 4, rank, width), BF16),
            pltpu.VMEM((2, rank, width), BF16),
            pltpu.VMEM((2, 2, rank, width), BF16),
            pltpu.VMEM((rank, width), BF16),
            pltpu.VMEM((rank, width), BF16),
            pltpu.VMEM((3, picks, value), BF16),
            pltpu.VMEM((7, rank, value), BF16),
            pltpu.VMEM((rows, value), F32),
            pltpu.VMEM((rows, 8 * half), BF16),
            pltpu.VMEM((4, 8, 128), F32),
            pltpu.VMEM((4 * picks, 8 * rank), BF16),
            pltpu.VMEM((rows, picks), BF16),
            pltpu.VMEM((rows, picks), BF16),
            pltpu.SemaphoreType.DMA((8,)),
            pltpu.SemaphoreType.DMA((NSEM,)),
            pltpu.SemaphoreType.DMA((NSEM,)),
        ],
        compiler_params=pltpu.CompilerParams(
            collective_id=0, has_side_effects=True, vmem_limit_bytes=56 * 2**20
        ),
        cost_estimate=pl.CostEstimate(
            flops=flops, bytes_accessed=4 * rows * model, transcendentals=0
        ),
    )(
        tokens,
        output_gradient,
        frozen_value_weight,
        adapter_down_maps,
        adapter_up_maps,
        block_tenant_ids,
        block_live_rows,
        tenant_owner_slot.reshape(1, -1),
    )
    return pl.pallas_call(
        copy_out,
        out_shape=shapes,
        in_specs=[hbm] * 4,
        compiler_params=pltpu.CompilerParams(vmem_limit_bytes=4 * 2**20),
        out_specs=(hbm,) * 4,
        scratch_shapes=[pltpu.SemaphoreType.DMA((COPY_PARTS + 3,))],
    )(*results)


def solution(mesh):
    placed = (
        P(("fsdp", "dp"), None),
        P(("fsdp", "dp"), None),
        P("fsdp", None),
        P(("fsdp", "dp"), None, None),
        P(("fsdp", "dp"), None, None),
        P(("fsdp", "dp")),
        P(("fsdp", "dp")),
        P(),
    )
    return jax.shard_map(
        on_device,
        mesh=mesh,
        in_specs=placed,
        out_specs=(
            P(("fsdp", "dp"), None),
            P(("fsdp", "dp"), None),
            P(("fsdp", "dp"), None, None),
            P(("fsdp", "dp"), None, None),
        ),
        check_vma=False,
    )
```
